32 devices in a mesh: freq: 4 (over y, x), tm: 8 (over z, core).
Axes of the slice: x: 2, y: 2, z: 4, core: 2. Of those that a mesh axis runs over, the one named last changes fastest.
Arguments:
- voltages: bfloat16 [2048, 530432], P(('tm', 'freq')), may hold values from -128 to 127, as said below
- fir_taps: float32 [4, 2048], replicated, may hold values from -3 to 3
Outputs:
- coherence: bfloat16 [2, 32, 2048, 2048], P(None, 'freq', 'tm')
The draws below stay inside these ranges and needn't reach their ends.
Inputs may be any that keep to these rules, and one draw needn't show every extreme that they name: `voltages`: every sample is a whole number.
All inputs are finite; a program needn't handle non-finite values.
Results may differ from the reference program's by a relative error of at most 0.0073.
Values may be sent and summed in bfloat16 or wider, within the bound.
No kernel may reach another device: no remote copies, remote signals or barrier semaphores. Data moves between devices by JAX's collectives and lax.ppermute only.
A program may use at most 384 MiB of HBM per device.

```python
import math
import jax
import jax.numpy as jnp
from jax import lax

A = 2048
P_SIZE = 2048
TAPS = 4
FIRST_BIN = 512
CH_DEV = 8
S = 256
SAMPLES = 530432
N_FREQ = 4


def draw_voltages(key, part):
    key_amp = jax.random.fold_in(key, 0)
    values = jax.random.randint(key_amp, (A, SAMPLES), -128, 128)
    return values.astype(jnp.float32).astype(jnp.bfloat16)


def gaussian(own_key, shape, deviation, limit, held_as=jnp.bfloat16):
    values = deviation * jax.random.normal(own_key, shape, jnp.float32)
    return jnp.clip(values, min=-limit, max=limit).astype(held_as)


def setup_inputs(seed: int = 0) -> dict:
    seeds = jax.random.split(jax.random.key(seed), 3)
    voltages = draw_voltages(jax.random.fold_in(seeds[2], 71), 0)
    fir_taps = gaussian(seeds[1], (TAPS, P_SIZE), 0.5, 3.0, jnp.float32)
    return {"voltages": voltages, "fir_taps": fir_taps}


def dft_table(channels):
    points = jnp.arange(P_SIZE, dtype=jnp.int32)
    bins = FIRST_BIN + jnp.arange(channels, dtype=jnp.int32)
    phase = points[:, None] * bins[None, :] % P_SIZE
    angle = 2.0 * math.pi / P_SIZE * phase.astype(jnp.float32)
    twiddle = jnp.stack([jnp.cos(angle), -jnp.sin(angle)], axis=2)
    return twiddle.reshape(P_SIZE, 2 * channels).astype(jnp.bfloat16)

def filter_frames(block, fir_taps):
    inputs_here = block.shape[0]
    samples = block.astype(jnp.float32).reshape(inputs_here, S + TAPS - 1, P_SIZE)
    frames = fir_taps[0] * samples[:, 0:S]
    for tap_index in range(1, TAPS):
        frames = frames + fir_taps[tap_index] * samples[:, tap_index:tap_index + S]
    return frames.astype(jnp.bfloat16).reshape(inputs_here * S, P_SIZE)

def reference(voltages, fir_taps):
    channels = CH_DEV * N_FREQ
    twiddle = dft_table(channels).astype(jnp.float32)
    group_count = 16
    blocked = voltages.reshape(group_count, A // group_count, SAMPLES)

    def channelize(block):
        frames = filter_frames(block, fir_taps).astype(jnp.float32)
        spectra = lax.dot_general(twiddle, frames, (((0,), (1,)), ((), ())), precision=lax.Precision.HIGHEST)
        return spectra.astype(jnp.bfloat16).reshape(channels, 2, block.shape[0], S)
    mapped = lax.map(channelize, blocked)
    spectra = jnp.transpose(mapped, (1, 2, 0, 3, 4)).reshape(channels, 2, A, S)
    wide = spectra.astype(jnp.float32)
    powers = lax.optimization_barrier(jnp.sum(wide * wide, axis=(1, 3))) / S + 1e-06

    def correlate(channel_data):
        chan_spectra, chan_powers = channel_data
        stacked = chan_spectra.reshape(2 * A, S)
        products = jnp.dot(stacked, stacked.T, precision=lax.Precision.HIGHEST).reshape(2, A, 2, A)
        real_part = products[0, :, 0] + products[1, :, 1]
        imag_part = products[1, :, 0] - products[0, :, 1]
        scale = lax.rsqrt(chan_powers)
        sums = jnp.stack([real_part, imag_part])
        return (sums * (scale / S)[None, :, None] * scale[None, None, :]).astype(jnp.bfloat16)
    result = lax.map(correlate, (wide, powers))
    return jnp.transpose(result, (1, 0, 2, 3))
```

```python
import functools
import math

import jax
import jax.numpy as jnp
from jax import lax
from jax.experimental import pallas as pl
from jax.experimental.pallas import tpu as pltpu
from jax.sharding import PartitionSpec as P

P_SIZE = 2048
TAPS = 4
FIRST_BIN = 512
CH_DEV = 8
S = 256
GROUP = 16
T_BLOCK = 37
CHUNK = 2


def folded_table(fir_taps, freq_count):
    channels = CH_DEV * freq_count
    points = jnp.arange(P_SIZE, dtype=jnp.int32)
    bins = FIRST_BIN + jnp.arange(channels, dtype=jnp.int32)
    phase = points[:, None] * bins[None, :] % P_SIZE
    angle = 2.0 * math.pi / P_SIZE * phase.astype(jnp.float32)
    twiddle = jnp.concatenate([jnp.cos(angle), -jnp.sin(angle)], axis=1)
    twiddle = twiddle.astype(jnp.bfloat16).astype(jnp.float32)
    folded = fir_taps.T[:, :, None] * twiddle[:, None, :]
    return folded.reshape(P_SIZE, TAPS * 2 * channels).astype(jnp.bfloat16)


def channelize_kernel(channels, x_ref, w_ref, o_ref, y_ref, u_ref, z_ref):
    step = pl.program_id(1)
    width = 2 * channels
    rows = jnp.concatenate(
        [x_ref[:, t * P_SIZE : (t + 1) * P_SIZE] for t in range(T_BLOCK)], axis=0
    )
    y = jnp.dot(rows, w_ref[...], preferred_element_type=jnp.float32)
    start = pl.multiple_of(step * T_BLOCK * GROUP, T_BLOCK * GROUP)
    y_ref[pl.ds(start, T_BLOCK * GROUP), :] = y

    @pl.when(step == pl.num_programs(1) - 1)
    def _():
        part = 32 * GROUP

        @pl.loop(0, S * GROUP // part)
        def _(i):
            base = i * part
            sums = {}
            for k in range(TAPS):
                lane, offset = k * width // 128 * 128, k * width % 128
                piece = y_ref[pl.ds(base + k * GROUP, part), lane : lane + max(width, 128)]
                sums[offset] = sums[offset] + piece if offset in sums else piece
            total = sums.pop(0)
            for offset, piece in sums.items():
                total = total + pltpu.roll(piece, 128 - offset, 1)
            u_ref[pl.ds(base, part), :] = total

        @pl.loop(0, GROUP)
        def _(a):
            spectra = u_ref[pl.ds(a, S, stride=GROUP), :].T
            real = spectra[:channels]
            imag = spectra[channels : 2 * channels]
            power = jnp.sum(real * real + imag * imag, axis=1, keepdims=True) / S + 1e-06
            scale = lax.rsqrt(power) * (1.0 / math.sqrt(S))
            for lane in range(0, S, 128):
                half = slice(lane, lane + 128)
                z_ref[lane // 128, pl.ds(a, channels, stride=GROUP), :] = real[:, half] * scale
                z_ref[(S + lane) // 128, pl.ds(a, channels, stride=GROUP), :] = imag[:, half] * scale

        for part in range(2 * S // 128):
            lanes = slice(part * 128, (part + 1) * 128)
            o_ref[:, :, lanes] = z_ref[part].astype(jnp.bfloat16).reshape(channels, GROUP, 128)


def channelize(voltages, table, freq_count):
    inputs_here, samples = voltages.shape
    channels = CH_DEV * freq_count
    columns = table.shape[1]
    groups = inputs_here // GROUP
    frames = samples // P_SIZE
    steps = frames // T_BLOCK
    return pl.pallas_call(
        functools.partial(channelize_kernel, channels),
        grid=(groups, steps),
        in_specs=[
            pl.BlockSpec((GROUP, T_BLOCK * P_SIZE), lambda g, t: (g, t)),
            pl.BlockSpec((P_SIZE, columns), lambda g, t: (0, 0)),
        ],
        out_specs=pl.BlockSpec((channels, GROUP, 2 * S), lambda g, t: (0, g, 0)),
        out_shape=jax.ShapeDtypeStruct((channels, inputs_here, 2 * S), jnp.bfloat16),
        scratch_shapes=[
            pltpu.VMEM((frames * GROUP, columns), jnp.float32),
            pltpu.VMEM((S * GROUP, max(128, 2 * channels)), jnp.float32),
            pltpu.VMEM((2 * S // 128, channels * GROUP, 128), jnp.float32),
        ],
        compiler_params=pltpu.CompilerParams(vmem_limit_bytes=48 * 1024 * 1024),
        cost_estimate=pl.CostEstimate(
            flops=2 * inputs_here * samples * columns,
            bytes_accessed=2 * inputs_here * samples,
            transcendentals=0,
        ),
        name="channelize",
    )(voltages, table)


def correlate(place, own, same, other, previous, first, total_columns):
    z_count, freq_count, chunk, block, depth = same.shape
    rows = freq_count * block
    slab = CH_DEV
    in_specs = [
        pl.BlockSpec((freq_count, None, block, depth), lambda c, p: (0, c, 0, 0)),
        pl.BlockSpec((z_count, freq_count, None, block, depth), lambda c, p: (0, 0, c, 0, 0)),
        pl.BlockSpec((z_count, freq_count, None, block, depth), lambda c, p: (0, 0, c, 0, 0)),
    ]
    args = [place, own, same, other]
    aliases = {}
    if previous is not None:
        in_specs.append(pl.BlockSpec(memory_space=pl.ANY))
        args.append(previous)
        aliases = {4: 0}

    def body(place_ref, own_ref, same_ref, other_ref, *rest):
        own = own_ref[...].reshape(rows, depth)
        core = place_ref[0]
        o_ref = rest[-1]
        turned = jnp.concatenate([own[:, S:], -own[:, :S]], axis=1)
        stacked = jnp.concatenate([own, turned], axis=0)
        for z in range(z_count):
            for source, parity in ((same_ref, core), (other_ref, 1 - core)):
                right = source[z].reshape(rows, depth)
                products = lax.dot_general(
                    stacked, right, (((1,), (1,)), ((), ())), preferred_element_type=jnp.float32
                ).astype(jnp.bfloat16)
                column = pl.multiple_of((2 * z + parity) * rows, rows)
                o_ref[0, 0, :, pl.ds(column, rows)] = products[:rows]
                o_ref[1, 0, :, pl.ds(column, rows)] = products[rows:]

    return pl.pallas_call(
        body,
        grid_spec=pltpu.PrefetchScalarGridSpec(
            num_scalar_prefetch=1,
            grid=(chunk,),
            in_specs=in_specs,
            out_specs=pl.BlockSpec(
                (2, 1, rows, total_columns), lambda c, p: (0, first + c, 0, 0)
            ),
        ),
        out_shape=jax.ShapeDtypeStruct((2, slab, rows, total_columns), jnp.bfloat16),
        input_output_aliases=aliases,
        compiler_params=pltpu.CompilerParams(vmem_limit_bytes=32 * 1024 * 1024),
        cost_estimate=pl.CostEstimate(
            flops=2 * chunk * 2 * rows * total_columns * depth,
            bytes_accessed=chunk * 2 * total_columns * (depth + 2 * rows),
            transcendentals=0,
        ),
        name="correlate",
    )(*args)


def on_device(voltages, fir_taps):
    freq_count = lax.axis_size("freq")
    tm_count = lax.axis_size("tm")
    inputs_here = voltages.shape[0]
    total_columns = inputs_here * freq_count * tm_count
    core = lax.axis_index("tm") % 2
    place = core.astype(jnp.int32).reshape(1)
    same_core = [list(range(c, tm_count, 2)) for c in range(2)]
    swap = [(i, i ^ 1) for i in range(tm_count)]

    table = folded_table(fir_taps, freq_count)
    spectra = channelize(voltages, table, freq_count)
    spectra = spectra.reshape(freq_count, CH_DEV, inputs_here, 2 * S)
    result = None
    for first in range(0, CH_DEV, CHUNK):
        piece = spectra[:, first : first + CHUNK]
        own = lax.all_to_all(piece, "freq", split_axis=0, concat_axis=0, tiled=True)
        same = lax.all_gather(own, "tm", axis=0, axis_index_groups=same_core)
        other = lax.ppermute(same, "tm", swap)
        result = correlate(place, own, same, other, result, first, total_columns)
    return result


def solution(mesh):
    placed = (P(("tm", "freq"), None), P())
    return jax.shard_map(
        on_device,
        mesh=mesh,
        in_specs=placed,
        out_specs=P(None, "freq", "tm", None),
        check_vma=False,
    )
```

```python
import functools
import math

import jax
import jax.numpy as jnp
from jax import lax
from jax.experimental import pallas as pl
from jax.experimental.pallas import tpu as pltpu
from jax.sharding import PartitionSpec as P

P_SIZE = 2048
TAPS = 4
FIRST_BIN = 512
CH_DEV = 8
S = 256
GROUP = 16
T_BLOCK = 37
T_PARTS = (13, 12, 12)
LANES = 128


def folded_table(fir_taps, freq_count):
    slabs = jnp.arange(freq_count, dtype=jnp.int32) ^ lax.axis_index("freq").astype(jnp.int32)
    channel = slabs[:, None] * CH_DEV + jnp.arange(CH_DEV, dtype=jnp.int32)[None, :]
    bins = FIRST_BIN + channel.reshape(-1)
    points = jnp.arange(P_SIZE, dtype=jnp.int32)
    phase = points[:, None] * bins[None, :] % P_SIZE
    angle = 2.0 * math.pi / P_SIZE * phase.astype(jnp.float32)
    twiddle = jnp.concatenate([jnp.cos(angle), -jnp.sin(angle)], axis=1)
    twiddle = twiddle.astype(jnp.bfloat16).astype(jnp.float32)
    folded = fir_taps.T[:, :, None] * twiddle[:, None, :]
    return folded.reshape(P_SIZE, -1).astype(jnp.bfloat16)


def channelize_kernel(channels, x_ref, w_ref, after_ref, o_ref, y_ref, u_ref, s_ref, z_ref):
    step = pl.program_id(0)
    width = 2 * channels
    halves = LANES // width
    depth = S // halves
    table = w_ref[...]
    done = 0
    for count in T_PARTS:
        rows = jnp.concatenate(
            [x_ref[:, t * P_SIZE : (t + 1) * P_SIZE] for t in range(done, done + count)], axis=0
        )
        start = pl.multiple_of((step * T_BLOCK + done) * GROUP, GROUP)
        y_ref[pl.ds(start, count * GROUP), :] = jnp.dot(
            rows, table, preferred_element_type=jnp.float32
        )
        done += count

    @pl.when(step == pl.num_programs(0) - 1)
    def _():
        part = 8

        def taps_sum(s, count):
            if halves == 1:
                total = y_ref[pl.ds(s * GROUP, count * GROUP), :LANES]
                for k in range(1, TAPS):
                    lanes = slice(k * LANES, (k + 1) * LANES)
                    total = total + y_ref[pl.ds((s + k) * GROUP, count * GROUP), lanes]
                return total
            low = y_ref[pl.ds(s * GROUP, count * GROUP), :LANES]
            return low + y_ref[pl.ds((s + 2) * GROUP, count * GROUP), LANES:]

        def combine(i, power):
            s = i * part
            size = part * GROUP
            if halves == 1:
                both = taps_sum(s, part)
            else:
                first = taps_sum(s, part + 1)
                second = taps_sum(s + depth, part + 1)
                lane = lax.broadcasted_iota(jnp.int32, (size, LANES), 1)
                low = first[:size] + pltpu.roll(first[GROUP:], width, 1)
                high = pltpu.roll(second[:size], width, 1) + second[GROUP:]
                both = jnp.where(lane < width, low, high)
            u_ref[pl.ds(pl.multiple_of(s * GROUP, size), size), :] = both
            return power + jnp.sum((both * both).reshape(part, GROUP, LANES), axis=0)

        power = lax.fori_loop(
            0, depth // part, combine, jnp.zeros((GROUP, LANES), jnp.float32)
        )
        shift = channels
        while shift < LANES:
            power = power + pltpu.roll(power, shift, 1)
            shift *= 2
        s_ref[...] = lax.rsqrt(power / S + 1e-06) * (1.0 / math.sqrt(S))

        per_half = depth // LANES
        for a in range(GROUP):
            spectra = (u_ref[pl.ds(a, depth, stride=GROUP), :] * s_ref[a : a + 1, :]).T
            for h in range(halves):
                for r in range(2):
                    first = (2 * h + r) * channels
                    for j in range(per_half):
                        z_ref[
                            r * (S // LANES) + h * per_half + j,
                            pl.ds(a, channels, stride=GROUP),
                            :,
                        ] = spectra[first : first + channels, j * LANES : (j + 1) * LANES]
        for part in range(2 * S // LANES):
            lanes = slice(part * LANES, (part + 1) * LANES)
            o_ref[:, :, lanes] = z_ref[part].astype(jnp.bfloat16).reshape(channels, GROUP, LANES)


def channelize(voltages, table, after, group):
    samples = voltages.shape[1]
    columns = table.shape[1]
    channels = columns // (2 * TAPS)
    frames = samples // P_SIZE
    return pl.pallas_call(
        functools.partial(channelize_kernel, channels),
        grid=(frames // T_BLOCK,),
        in_specs=[
            pl.BlockSpec((GROUP, T_BLOCK * P_SIZE), lambda t: (group, t)),
            pl.BlockSpec((P_SIZE, columns), lambda t: (0, 0)),
            pl.BlockSpec(memory_space=pl.ANY),
        ],
        out_specs=pl.BlockSpec((channels, GROUP, 2 * S), lambda t: (0, 0, 0)),
        out_shape=jax.ShapeDtypeStruct((channels, GROUP, 2 * S), jnp.bfloat16),
        scratch_shapes=[
            pltpu.VMEM((frames * GROUP, columns), jnp.float32),
            pltpu.VMEM((S * 2 * channels // LANES * GROUP, LANES), jnp.float32),
            pltpu.VMEM((GROUP, LANES), jnp.float32),
            pltpu.VMEM((2 * S // LANES, channels * GROUP, LANES), jnp.float32),
        ],
        compiler_params=pltpu.CompilerParams(vmem_limit_bytes=40 * 1024 * 1024),
        cost_estimate=pl.CostEstimate(
            flops=2 * GROUP * samples * columns,
            bytes_accessed=2 * GROUP * samples,
            transcendentals=0,
        ),
        name="channelize",
    )(voltages, table, after)


def correlate_kernel(groups, place_ref, *refs):
    o_ref, token_ref = refs[-2:]
    token_ref[...] = jnp.zeros_like(token_ref)
    own, same, other = (refs[i * groups : (i + 1) * groups] for i in range(3))
    freq_count = own[0].shape[0]
    freq, core = place_ref[0], place_ref[1]
    rows = freq_count * groups * GROUP

    def inputs_of(sources):
        return jnp.concatenate(
            [source[f ^ freq] for f in range(freq_count) for source in sources], axis=0
        )

    left = inputs_of(own)
    turned = jnp.concatenate([left[:, S:], -left[:, :S]], axis=1)
    stacked = jnp.concatenate([left, turned], axis=0)
    for sources, parity in ((same, core), (other, 1 - core)):
        products = lax.dot_general(
            stacked,
            inputs_of(sources),
            (((1,), (1,)), ((), ())),
            preferred_element_type=jnp.float32,
        ).astype(jnp.bfloat16)
        column = pl.multiple_of(parity * rows, rows)
        o_ref[0, :, pl.ds(column, rows)] = products[:rows]
        o_ref[1, :, pl.ds(column, rows)] = products[rows:]


def correlate(place, own, same, other, previous, total_columns):
    groups = len(own)
    freq_count, slab, block, depth = own[0].shape
    rows = freq_count * groups * block
    piece = pl.BlockSpec((freq_count, None, block, depth), lambda c, p: (0, c, 0, 0))
    in_specs = [piece] * (3 * groups)
    args = [place, *own, *same, *other]
    aliases = {}
    if previous is not None:
        aliases = {len(args): 0}
        in_specs.append(pl.BlockSpec(memory_space=pl.ANY))
        args.append(previous)
    return pl.pallas_call(
        functools.partial(correlate_kernel, groups),
        grid_spec=pltpu.PrefetchScalarGridSpec(
            num_scalar_prefetch=1,
            grid=(slab,),
            in_specs=in_specs,
            out_specs=[
                pl.BlockSpec((2, None, rows, 2 * rows), lambda c, p: (0, c, 0, p[2])),
                pl.BlockSpec((8, LANES), lambda c, p: (0, 0)),
            ],
        ),
        out_shape=[
            jax.ShapeDtypeStruct((2, slab, rows, total_columns), jnp.bfloat16),
            jax.ShapeDtypeStruct((8, LANES), jnp.float32),
        ],
        input_output_aliases=aliases,
        compiler_params=pltpu.CompilerParams(vmem_limit_bytes=32 * 1024 * 1024),
        cost_estimate=pl.CostEstimate(
            flops=2 * slab * 2 * rows * 2 * rows * depth,
            bytes_accessed=slab * 2 * rows * (3 * depth + 4 * rows),
            transcendentals=0,
        ),
        name="correlate",
    )(*args)


def on_device(voltages, fir_taps):
    freq_count = lax.axis_size("freq")
    tm_count = lax.axis_size("tm")
    inputs_here = voltages.shape[0]
    total_columns = inputs_here * freq_count * tm_count
    groups = inputs_here // GROUP
    ring = tm_count // 2
    tm = lax.axis_index("tm").astype(jnp.int32)
    freq = lax.axis_index("freq").astype(jnp.int32)
    swap = [(i, i ^ 1) for i in range(tm_count)]
    onward = [(i, (i + 2) % tm_count) for i in range(tm_count)]

    table = folded_table(fir_taps, freq_count)
    token = jnp.zeros((8, LANES), jnp.float32)
    held = [[None] * groups for _ in range(ring)]

    def after(token, *arrays):
        return lax.optimization_barrier((token, *arrays))

    def move_on(step, group, token=None):
        piece = held[step - 1][group]
        if token is not None:
            piece, _ = lax.optimization_barrier((piece, token))
        held[step][group] = lax.ppermute(piece, "tm", onward)

    for group in range(groups):
        if group == 2:
            token, held[0][0] = after(token, held[0][0])
        elif group >= 3:
            if held[1][group - 3] is None:
                move_on(1, group - 3)
            token, held[0][group - 2], held[0][group - 1], held[1][group - 3] = after(
                token, held[0][group - 2], held[0][group - 1], held[1][group - 3]
            )
        spectra = channelize(voltages, table, token, group)
        token, spectra = after(token, spectra)
        if group == groups - 1 and groups >= 4 and ring >= 3:
            move_on(1, group - 2)
            move_on(2, group - 3)
            spectra, held[1][group - 2], held[2][group - 3] = lax.optimization_barrier(
                (spectra, held[1][group - 2], held[2][group - 3])
            )
        spectra = spectra.reshape(freq_count, CH_DEV, GROUP, 2 * S)
        parts = [spectra[0]]
        for k in range(1, freq_count):
            partners = [(i, i ^ k) for i in range(freq_count)]
            parts.append(lax.ppermute(spectra[k], "freq", partners))
        held[0][group] = jnp.stack(parts)

    result, tokens = None, []
    for step in range(ring):
        for group in range(groups):
            if held[step][group] is None:
                late = step >= 2 and group >= groups // 2
                move_on(step, group, tokens[step - 2] if late else None)
        other = []
        for group in range(groups):
            piece = held[step][group]
            if step == ring - 1 and step >= 1 and group >= groups // 2:
                piece, _ = lax.optimization_barrier((piece, tokens[step - 1]))
            other.append(lax.ppermute(piece, "tm", swap))
        source = (tm // 2 + ring - step) % ring
        place = jnp.stack([freq, tm % 2, source])
        result, token = correlate(place, held[0], held[step], other, result, total_columns)
        tokens.append(token)
    return result


def solution(mesh):
    placed = (P(("tm", "freq"), None), P())
    return jax.shard_map(
        on_device,
        mesh=mesh,
        in_specs=placed,
        out_specs=P(None, "freq", "tm", None),
        check_vma=False,
    )
```

```python
import functools
import math

import jax
import jax.numpy as jnp
from jax import lax
from jax.experimental import pallas as pl
from jax.experimental.pallas import tpu as pltpu
from jax.sharding import PartitionSpec as P

P_SIZE = 2048
TAPS = 4
FIRST_BIN = 512
CH_DEV = 8
S = 256
GROUP = 16
T_BLOCK = 37
T_PARTS = (13, 12, 12)
LANES = 128


def folded_table(fir_taps, freq_count):
    slabs = jnp.arange(freq_count, dtype=jnp.int32) ^ lax.axis_index("freq").astype(jnp.int32)
    channel = slabs[:, None] * CH_DEV + jnp.arange(CH_DEV, dtype=jnp.int32)[None, :]
    bins = FIRST_BIN + channel.reshape(-1)
    points = jnp.arange(P_SIZE, dtype=jnp.int32)
    phase = points[:, None] * bins[None, :] % P_SIZE
    angle = 2.0 * math.pi / P_SIZE * phase.astype(jnp.float32)
    twiddle = jnp.concatenate([jnp.cos(angle), -jnp.sin(angle)], axis=1)
    twiddle = twiddle.astype(jnp.bfloat16).astype(jnp.float32)
    folded = fir_taps.T[:, :, None] * twiddle[:, None, :]
    return folded.reshape(P_SIZE, -1).astype(jnp.bfloat16)


def channelize_kernel(channels, x_ref, w_ref, after_ref, o_ref, y_ref, u_ref, s_ref, z_ref):
    step = pl.program_id(0)
    width = 2 * channels
    halves = LANES // width
    depth = S // halves
    table = w_ref[...]
    done = 0
    for count in T_PARTS:
        rows = jnp.concatenate(
            [x_ref[:, t * P_SIZE : (t + 1) * P_SIZE] for t in range(done, done + count)], axis=0
        )
        start = pl.multiple_of((step * T_BLOCK + done) * GROUP, GROUP)
        y_ref[pl.ds(start, count * GROUP), :] = jnp.dot(
            rows, table, preferred_element_type=jnp.float32
        )
        done += count

    @pl.when(step == pl.num_programs(0) - 1)
    def _():
        part = 8

        def taps_sum(s, count):
            if halves == 1:
                total = y_ref[pl.ds(s * GROUP, count * GROUP), :LANES]
                for k in range(1, TAPS):
                    lanes = slice(k * LANES, (k + 1) * LANES)
                    total = total + y_ref[pl.ds((s + k) * GROUP, count * GROUP), lanes]
                return total
            low = y_ref[pl.ds(s * GROUP, count * GROUP), :LANES]
            return low + y_ref[pl.ds((s + 2) * GROUP, count * GROUP), LANES:]

        def combine(i, power):
            s = i * part
            size = part * GROUP
            if halves == 1:
                both = taps_sum(s, part)
            else:
                first = taps_sum(s, part + 1)
                second = taps_sum(s + depth, part + 1)
                lane = lax.broadcasted_iota(jnp.int32, (size, LANES), 1)
                low = first[:size] + pltpu.roll(first[GROUP:], width, 1)
                high = pltpu.roll(second[:size], width, 1) + second[GROUP:]
                both = jnp.where(lane < width, low, high)
            u_ref[pl.ds(pl.multiple_of(s * GROUP, size), size), :] = both
            return power + jnp.sum((both * both).reshape(part, GROUP, LANES), axis=0)

        power = lax.fori_loop(
            0, depth // part, combine, jnp.zeros((GROUP, LANES), jnp.float32)
        )
        shift = channels
        while shift < LANES:
            power = power + pltpu.roll(power, shift, 1)
            shift *= 2
        s_ref[...] = lax.rsqrt(power / S + 1e-06) * (1.0 / math.sqrt(S))

        per_half = depth // LANES
        for a in range(GROUP):
            spectra = (u_ref[pl.ds(a, depth, stride=GROUP), :] * s_ref[a : a + 1, :]).T
            for h in range(halves):
                for r in range(2):
                    first = (2 * h + r) * channels
                    for j in range(per_half):
                        z_ref[
                            r * (S // LANES) + h * per_half + j,
                            pl.ds(a, channels, stride=GROUP),
                            :,
                        ] = spectra[first : first + channels, j * LANES : (j + 1) * LANES]
        for part in range(2 * S // LANES):
            lanes = slice(part * LANES, (part + 1) * LANES)
            o_ref[:, :, lanes] = z_ref[part].astype(jnp.bfloat16).reshape(channels, GROUP, LANES)


def channelize(voltages, table, after, group):
    samples = voltages.shape[1]
    columns = table.shape[1]
    channels = columns // (2 * TAPS)
    frames = samples // P_SIZE
    return pl.pallas_call(
        functools.partial(channelize_kernel, channels),
        grid=(frames // T_BLOCK,),
        in_specs=[
            pl.BlockSpec((GROUP, T_BLOCK * P_SIZE), lambda t: (group, t)),
            pl.BlockSpec((P_SIZE, columns), lambda t: (0, 0)),
            pl.BlockSpec(memory_space=pl.ANY),
        ],
        out_specs=pl.BlockSpec((channels, GROUP, 2 * S), lambda t: (0, 0, 0)),
        out_shape=jax.ShapeDtypeStruct((channels, GROUP, 2 * S), jnp.bfloat16),
        scratch_shapes=[
            pltpu.VMEM((frames * GROUP, columns), jnp.float32),
            pltpu.VMEM((S * 2 * channels // LANES * GROUP, LANES), jnp.float32),
            pltpu.VMEM((GROUP, LANES), jnp.float32),
            pltpu.VMEM((2 * S // LANES, channels * GROUP, LANES), jnp.float32),
        ],
        compiler_params=pltpu.CompilerParams(vmem_limit_bytes=40 * 1024 * 1024),
        cost_estimate=pl.CostEstimate(
            flops=2 * GROUP * samples * columns,
            bytes_accessed=2 * GROUP * samples,
            transcendentals=0,
        ),
        name="channelize",
    )(voltages, table, after)


def correlate_kernel(groups, place_ref, *refs):
    o_ref, token_ref = refs[-2:]
    token_ref[...] = jnp.zeros_like(token_ref)
    own, same, other = (refs[i * groups : (i + 1) * groups] for i in range(3))
    freq_count = own[0].shape[0]
    freq, core = place_ref[0], place_ref[1]
    rows = freq_count * groups * GROUP

    def inputs_of(sources):
        return jnp.concatenate(
            [source[f ^ freq] for f in range(freq_count) for source in sources], axis=0
        )

    left = inputs_of(own)
    turned = jnp.concatenate([left[:, S:], -left[:, :S]], axis=1)
    stacked = jnp.concatenate([left, turned], axis=0)
    for sources, parity in ((same, core), (other, 1 - core)):
        products = lax.dot_general(
            stacked,
            inputs_of(sources),
            (((1,), (1,)), ((), ())),
            preferred_element_type=jnp.float32,
        ).astype(jnp.bfloat16)
        column = pl.multiple_of(parity * rows, rows)
        o_ref[0, :, pl.ds(column, rows)] = products[:rows]
        o_ref[1, :, pl.ds(column, rows)] = products[rows:]


def correlate(place, own, same, other, previous, total_columns):
    groups = len(own)
    freq_count, slab, block, depth = own[0].shape
    rows = freq_count * groups * block
    piece = pl.BlockSpec((freq_count, None, block, depth), lambda c, p: (0, c, 0, 0))
    in_specs = [piece] * (3 * groups)
    args = [place, *own, *same, *other]
    aliases = {}
    if previous is not None:
        aliases = {len(args): 0}
        in_specs.append(pl.BlockSpec(memory_space=pl.ANY))
        args.append(previous)
    return pl.pallas_call(
        functools.partial(correlate_kernel, groups),
        grid_spec=pltpu.PrefetchScalarGridSpec(
            num_scalar_prefetch=1,
            grid=(slab,),
            in_specs=in_specs,
            out_specs=[
                pl.BlockSpec((2, None, rows, 2 * rows), lambda c, p: (0, c, 0, p[2])),
                pl.BlockSpec((8, LANES), lambda c, p: (0, 0)),
            ],
        ),
        out_shape=[
            jax.ShapeDtypeStruct((2, slab, rows, total_columns), jnp.bfloat16),
            jax.ShapeDtypeStruct((8, LANES), jnp.float32),
        ],
        input_output_aliases=aliases,
        compiler_params=pltpu.CompilerParams(vmem_limit_bytes=32 * 1024 * 1024),
        cost_estimate=pl.CostEstimate(
            flops=2 * slab * 2 * rows * 2 * rows * depth,
            bytes_accessed=slab * 2 * rows * (3 * depth + 4 * rows),
            transcendentals=0,
        ),
        name="correlate",
    )(*args)


def on_device(voltages, fir_taps):
    freq_count = lax.axis_size("freq")
    tm_count = lax.axis_size("tm")
    inputs_here = voltages.shape[0]
    total_columns = inputs_here * freq_count * tm_count
    groups = inputs_here // GROUP
    ring = tm_count // 2
    tm = lax.axis_index("tm").astype(jnp.int32)
    freq = lax.axis_index("freq").astype(jnp.int32)
    swap = [(i, i ^ 1) for i in range(tm_count)]
    onward = [(i, (i + 2) % tm_count) for i in range(tm_count)]

    table = folded_table(fir_taps, freq_count)
    token = jnp.zeros((8, LANES), jnp.float32)
    held, swapped = {}, {}

    def behind(array, *others):
        for other in others:
            array, _ = lax.optimization_barrier((array, other))
        return array

    def move_on(step, group, *others):
        if (step, group) not in held:
            piece = behind(held[step - 1, group], *others)
            held[step, group] = lax.ppermute(piece, "tm", onward)
        return held[step, group]

    def swap_cores(step, group, *others):
        if (step, group) not in swapped:
            piece = behind(held[step, group], *others)
            swapped[step, group] = lax.ppermute(piece, "tm", swap)
        return swapped[step, group]

    for group in range(groups):
        if group:
            token = behind(token, held[0, group - 1])
        spectra = channelize(voltages, table, token, group)
        if group:
            spectra = behind(
                spectra,
                swap_cores(0, group - 1),
                *([move_on(group, 0)] if group < ring else []),
                *([move_on(1, group - 1)] if ring > 1 else []),
            )
        spectra = spectra.reshape(freq_count, CH_DEV, GROUP, 2 * S)
        parts = [spectra[0]]
        for k in range(1, freq_count):
            partners = [(i, i ^ k) for i in range(freq_count)]
            parts.append(lax.ppermute(spectra[k], "freq", partners))
        if group >= 3 and ring > 2:
            parts[-1] = behind(parts[-1], move_on(2, group - 2))
        held[0, group] = jnp.stack(parts)

    result, tokens = None, []
    for step in range(ring):
        for group in range(groups):
            others = []
            if step >= 2 and group == groups - 1:
                others.append(tokens[step - 2])
            if step >= 2 and group >= 1:
                others.append(swap_cores(step - 1, group - 1))
            move_on(step, group, *others)
        for group in range(groups):
            late = step == ring - 1 and step >= 1 and group >= groups // 2
            swap_cores(step, group, *([tokens[step - 1]] if late else []))
        source = (tm // 2 + ring - step) % ring
        place = jnp.stack([freq, tm % 2, source])
        result, token = correlate(
            place,
            [held[0, group] for group in range(groups)],
            [held[step, group] for group in range(groups)],
            [swapped[step, group] for group in range(groups)],
            result,
            total_columns,
        )
        tokens.append(token)
    return result


def solution(mesh):
    placed = (P(("tm", "freq"), None), P())
    return jax.shard_map(
        on_device,
        mesh=mesh,
        in_specs=placed,
        out_specs=P(None, "freq", "tm", None),
        check_vma=False,
    )
```

```python
import functools
import math

import jax
import jax.numpy as jnp
from jax import lax
from jax.experimental import pallas as pl
from jax.experimental.pallas import tpu as pltpu
from jax.sharding import PartitionSpec as P

P_SIZE = 2048
TAPS = 4
FIRST_BIN = 512
CH_DEV = 8
S = 256
GROUP = 16
T_BLOCK = 37
MXU = 256
LANES = 128


def folded_table(fir_taps, freq_count):
    slabs = jnp.arange(freq_count, dtype=jnp.int32) ^ lax.axis_index("freq").astype(jnp.int32)
    channel = slabs[:, None] * CH_DEV + jnp.arange(CH_DEV, dtype=jnp.int32)[None, :]
    bins = FIRST_BIN + channel.reshape(-1)
    points = jnp.arange(P_SIZE, dtype=jnp.int32)
    phase = points[:, None] * bins[None, :] % P_SIZE
    angle = 2.0 * math.pi / P_SIZE * phase.astype(jnp.float32)
    twiddle = jnp.concatenate([jnp.cos(angle), -jnp.sin(angle)], axis=1)
    twiddle = twiddle.astype(jnp.bfloat16).astype(jnp.float32)
    folded = fir_taps.T[:, :, None] * twiddle[:, None, :]
    return folded.reshape(P_SIZE, -1).astype(jnp.bfloat16)


def unit_shares(columns):
    if columns == MXU:
        half = T_BLOCK // 2
        return [(0, half, 0), (half, T_BLOCK, 0)]
    return [(0, T_BLOCK, 0), (0, T_BLOCK, MXU)]


def channelize_kernel(channels, x_ref, w_ref, after_ref, o_ref, y_ref, u_ref, s_ref, z_ref):
    step = pl.program_id(0)
    width = 2 * channels
    halves = LANES // width
    depth = S // halves
    shares = unit_shares(w_ref.shape[1])

    def multiply(*sums):
        for k in range(P_SIZE // MXU):
            depths = slice(k * MXU, (k + 1) * MXU)
            for unit, (begin, end, column) in enumerate(shares):
                pltpu.matmul_push_rhs(w_ref[depths, column : column + MXU], k % 2, unit)
            for unit, (begin, end, column) in enumerate(shares):
                rows = jnp.concatenate(
                    [
                        x_ref[:, t * P_SIZE + k * MXU : t * P_SIZE + (k + 1) * MXU]
                        for t in range(begin, end)
                    ],
                    axis=0,
                )
                pltpu.matmul_acc_lhs(sums[unit], rows, load_staged_rhs=k % 2)
        for unit, (begin, end, column) in enumerate(shares):
            start = pl.multiple_of((step * T_BLOCK + begin) * GROUP, GROUP)
            y_ref[pl.ds(start, (end - begin) * GROUP), column : column + MXU] = (
                pltpu.matmul_pop(sums[unit])
            )

    pl.run_scoped(
        multiply,
        *[
            pltpu.ACC(unit)(((end - begin) * GROUP, MXU), jnp.float32)
            for unit, (begin, end, column) in enumerate(shares)
        ],
    )

    @pl.when(step == pl.num_programs(0) - 1)
    def _():
        part = 8

        def taps_sum(s, count):
            if halves == 1:
                total = y_ref[pl.ds(s * GROUP, count * GROUP), :LANES]
                for k in range(1, TAPS):
                    lanes = slice(k * LANES, (k + 1) * LANES)
                    total = total + y_ref[pl.ds((s + k) * GROUP, count * GROUP), lanes]
                return total
            low = y_ref[pl.ds(s * GROUP, count * GROUP), :LANES]
            return low + y_ref[pl.ds((s + 2) * GROUP, count * GROUP), LANES:]

        def combine(i, power):
            s = i * part
            size = part * GROUP
            if halves == 1:
                both = taps_sum(s, part)
            else:
                first = taps_sum(s, part + 1)
                second = taps_sum(s + depth, part + 1)
                lane = lax.broadcasted_iota(jnp.int32, (size, LANES), 1)
                low = first[:size] + pltpu.roll(first[GROUP:], width, 1)
                high = pltpu.roll(second[:size], width, 1) + second[GROUP:]
                both = jnp.where(lane < width, low, high)
            u_ref[pl.ds(pl.multiple_of(s * GROUP, size), size), :] = both
            return power + jnp.sum((both * both).reshape(part, GROUP, LANES), axis=0)

        power = lax.fori_loop(
            0, depth // part, combine, jnp.zeros((GROUP, LANES), jnp.float32)
        )
        shift = channels
        while shift < LANES:
            power = power + pltpu.roll(power, shift, 1)
            shift *= 2
        s_ref[...] = lax.rsqrt(power / S + 1e-06) * (1.0 / math.sqrt(S))

        per_half = depth // LANES
        for a in range(GROUP):
            spectra = (u_ref[pl.ds(a, depth, stride=GROUP), :] * s_ref[a : a + 1, :]).T
            for h in range(halves):
                for r in range(2):
                    first = (2 * h + r) * channels
                    for j in range(per_half):
                        z_ref[
                            r * (S // LANES) + h * per_half + j,
                            pl.ds(a, channels, stride=GROUP),
                            :,
                        ] = spectra[first : first + channels, j * LANES : (j + 1) * LANES]
        for part in range(2 * S // LANES):
            lanes = slice(part * LANES, (part + 1) * LANES)
            o_ref[:, :, lanes] = z_ref[part].astype(jnp.bfloat16).reshape(channels, GROUP, LANES)


def channelize(voltages, table, after, group):
    samples = voltages.shape[1]
    columns = table.shape[1]
    channels = columns // (2 * TAPS)
    frames = samples // P_SIZE
    return pl.pallas_call(
        functools.partial(channelize_kernel, channels),
        grid=(frames // T_BLOCK,),
        in_specs=[
            pl.BlockSpec((GROUP, T_BLOCK * P_SIZE), lambda t: (group, t)),
            pl.BlockSpec((P_SIZE, columns), lambda t: (0, 0)),
            pl.BlockSpec(memory_space=pl.ANY),
        ],
        out_specs=pl.BlockSpec((channels, GROUP, 2 * S), lambda t: (0, 0, 0)),
        out_shape=jax.ShapeDtypeStruct((channels, GROUP, 2 * S), jnp.bfloat16),
        scratch_shapes=[
            pltpu.VMEM((frames * GROUP, columns), jnp.float32),
            pltpu.VMEM((S * 2 * channels // LANES * GROUP, LANES), jnp.float32),
            pltpu.VMEM((GROUP, LANES), jnp.float32),
            pltpu.VMEM((2 * S // LANES, channels * GROUP, LANES), jnp.float32),
        ],
        compiler_params=pltpu.CompilerParams(vmem_limit_bytes=40 * 1024 * 1024),
        cost_estimate=pl.CostEstimate(
            flops=2 * GROUP * samples * columns,
            bytes_accessed=2 * GROUP * samples,
            transcendentals=0,
        ),
        name="channelize",
    )(voltages, table, after)


def correlate_kernel(groups, place_ref, *refs):
    o_ref, token_ref = refs[-2:]
    token_ref[...] = jnp.zeros_like(token_ref)
    own, same, other = (refs[i * groups : (i + 1) * groups] for i in range(3))
    freq_count = own[0].shape[0]
    freq, core = place_ref[0], place_ref[1]
    rows = freq_count * groups * GROUP

    def inputs_of(sources):
        return jnp.concatenate(
            [source[f ^ freq] for f in range(freq_count) for source in sources], axis=0
        )

    left = inputs_of(own)
    turned = jnp.concatenate([left[:, S:], -left[:, :S]], axis=1)
    stacked = jnp.concatenate([left, turned], axis=0)
    rights = [inputs_of(same), inputs_of(other)]

    def keep(products, parity):
        products = products.astype(jnp.bfloat16)
        column = pl.multiple_of(parity * rows, rows)
        o_ref[0, :, pl.ds(column, rows)] = products[:rows]
        o_ref[1, :, pl.ds(column, rows)] = products[rows:]

    def multiply(*sums):
        for k in range(2 * S // MXU):
            depths = slice(k * MXU, (k + 1) * MXU)
            for unit, right in enumerate(rights):
                pltpu.matmul_push_rhs(right[:, depths], k % 2, unit, transpose=True)
            for unit in range(2):
                pltpu.matmul_acc_lhs(sums[unit], stacked[:, depths], load_staged_rhs=k % 2)
        for unit, parity in enumerate((core, 1 - core)):
            keep(pltpu.matmul_pop(sums[unit]), parity)

    if rows == MXU:
        pl.run_scoped(
            multiply, *[pltpu.ACC(unit)((2 * rows, MXU), jnp.float32) for unit in range(2)]
        )
    else:
        for right, parity in zip(rights, (core, 1 - core)):
            products = lax.dot_general(
                stacked, right, (((1,), (1,)), ((), ())), preferred_element_type=jnp.float32
            )
            keep(products, parity)


def correlate(place, own, same, other, previous, total_columns):
    groups = len(own)
    freq_count, slab, block, depth = own[0].shape
    rows = freq_count * groups * block
    piece = pl.BlockSpec((freq_count, None, block, depth), lambda c, p: (0, c, 0, 0))
    in_specs = [piece] * (3 * groups)
    args = [place, *own, *same, *other]
    aliases = {}
    if previous is not None:
        aliases = {len(args): 0}
        in_specs.append(pl.BlockSpec(memory_space=pl.ANY))
        args.append(previous)
    return pl.pallas_call(
        functools.partial(correlate_kernel, groups),
        grid_spec=pltpu.PrefetchScalarGridSpec(
            num_scalar_prefetch=1,
            grid=(slab,),
            in_specs=in_specs,
            out_specs=[
                pl.BlockSpec((2, None, rows, 2 * rows), lambda c, p: (0, c, 0, p[2])),
                pl.BlockSpec((8, LANES), lambda c, p: (0, 0)),
            ],
        ),
        out_shape=[
            jax.ShapeDtypeStruct((2, slab, rows, total_columns), jnp.bfloat16),
            jax.ShapeDtypeStruct((8, LANES), jnp.float32),
        ],
        input_output_aliases=aliases,
        compiler_params=pltpu.CompilerParams(vmem_limit_bytes=32 * 1024 * 1024),
        cost_estimate=pl.CostEstimate(
            flops=2 * slab * 2 * rows * 2 * rows * depth,
            bytes_accessed=slab * 2 * rows * (3 * depth + 4 * rows),
            transcendentals=0,
        ),
        name="correlate",
    )(*args)


def on_device(voltages, fir_taps):
    freq_count = lax.axis_size("freq")
    tm_count = lax.axis_size("tm")
    inputs_here = voltages.shape[0]
    total_columns = inputs_here * freq_count * tm_count
    groups = inputs_here // GROUP
    ring = tm_count // 2
    tm = lax.axis_index("tm").astype(jnp.int32)
    freq = lax.axis_index("freq").astype(jnp.int32)
    swap = [(i, i ^ 1) for i in range(tm_count)]
    onward = [(i, (i + 2) % tm_count) for i in range(tm_count)]

    table = folded_table(fir_taps, freq_count)
    token = jnp.zeros((8, LANES), jnp.float32)
    held, swapped = {}, {}

    def behind(array, *others):
        for other in others:
            array, _ = lax.optimization_barrier((array, other))
        return array

    def move_on(step, group, *others):
        if (step, group) not in held:
            piece = behind(held[step - 1, group], *others)
            held[step, group] = lax.ppermute(piece, "tm", onward)
        return held[step, group]

    def swap_cores(step, group, *others):
        if (step, group) not in swapped:
            piece = behind(held[step, group], *others)
            swapped[step, group] = lax.ppermute(piece, "tm", swap)
        return swapped[step, group]

    deep = groups == 4 and ring >= 3
    for group in range(groups):
        if deep and group == 2:
            token = behind(token, held[0, 0])
        if deep and group == 3:
            token = behind(token, held[0, 1], held[0, 2], move_on(1, 0))
        spectra = channelize(voltages, table, token, group)
        token = behind(token, spectra)
        if deep and group == 3:
            closed = [swap_cores(0, 0), swap_cores(0, 1)]
            spectra = behind(spectra, move_on(1, 1), move_on(2, 0), *closed)
        spectra = spectra.reshape(freq_count, CH_DEV, GROUP, 2 * S)
        parts = [spectra[0]]
        for k in range(1, freq_count):
            partners = [(i, i ^ k) for i in range(freq_count)]
            parts.append(lax.ppermute(spectra[k], "freq", partners))
        if deep and group == 3:
            parts[-1] = behind(parts[-1], move_on(1, 2))
        held[0, group] = jnp.stack(parts)

    result, tokens = None, []
    for step in range(ring):
        for group in range(groups):
            others = []
            if step >= 2 and group == groups - 1:
                others.append(tokens[step - 2])
            if step >= 2 and group >= 1:
                others.append(swap_cores(step - 1, group - 1))
            move_on(step, group, *others)
        for group in range(groups):
            late = step == ring - 1 and step >= 1 and group >= groups // 2
            swap_cores(step, group, *([tokens[step - 1]] if late else []))
        source = (tm // 2 + ring - step) % ring
        place = jnp.stack([freq, tm % 2, source])
        result, token = correlate(
            place,
            [held[0, group] for group in range(groups)],
            [held[step, group] for group in range(groups)],
            [swapped[step, group] for group in range(groups)],
            result,
            total_columns,
        )
        tokens.append(token)
    return result


def solution(mesh):
    placed = (P(("tm", "freq"), None), P())
    return jax.shard_map(
        on_device,
        mesh=mesh,
        in_specs=placed,
        out_specs=P(None, "freq", "tm", None),
        check_vma=False,
    )
```

```python
import functools
import math

import jax
import jax.numpy as jnp
from jax import lax
from jax.experimental import pallas as pl
from jax.experimental.pallas import tpu as pltpu
from jax.sharding import PartitionSpec as P

P_SIZE = 2048
TAPS = 4
FIRST_BIN = 512
CH_DEV = 8
S = 256
GROUP = 16
T_BLOCK = 37
MXU = 256
LANES = 128


def folded_table(fir_taps, freq_count):
    slabs = jnp.arange(freq_count, dtype=jnp.int32) ^ lax.axis_index("freq").astype(jnp.int32)
    channel = slabs[:, None] * CH_DEV + jnp.arange(CH_DEV, dtype=jnp.int32)[None, :]
    bins = FIRST_BIN + channel.reshape(-1)
    points = jnp.arange(P_SIZE, dtype=jnp.int32)
    phase = points[:, None] * bins[None, :] % P_SIZE
    angle = 2.0 * math.pi / P_SIZE * phase.astype(jnp.float32)
    twiddle = jnp.concatenate([jnp.cos(angle), -jnp.sin(angle)], axis=1)
    twiddle = twiddle.astype(jnp.bfloat16).astype(jnp.float32)
    folded = fir_taps.T[:, :, None] * twiddle[:, None, :]
    return folded.reshape(P_SIZE, -1).astype(jnp.bfloat16)


def joined(pieces):
    return jnp.concatenate([piece.astype(jnp.float32) for piece in pieces], axis=0)


def unit_shares(columns):
    if columns == MXU:
        half = T_BLOCK // 2
        return [(0, half, 0), (half, T_BLOCK, 0)]
    return [(0, T_BLOCK, 0), (0, T_BLOCK, MXU)]


def channelize_kernel(channels, x_ref, w_ref, after_ref, o_ref, y_ref, u_ref, s_ref, z_ref):
    step = pl.program_id(1)
    width = 2 * channels
    halves = LANES // width
    depth = S // halves
    shares = unit_shares(w_ref.shape[1])

    def multiply(*sums):
        for k in range(P_SIZE // MXU):
            depths = slice(k * MXU, (k + 1) * MXU)
            for unit, (begin, end, column) in enumerate(shares):
                pltpu.matmul_push_rhs(w_ref[depths, column : column + MXU], k % 2, unit)
            for unit, (begin, end, column) in enumerate(shares):
                rows = joined(
                    [
                        x_ref[:, t * P_SIZE + k * MXU : t * P_SIZE + (k + 1) * MXU]
                        for t in range(begin, end)
                    ]
                )
                pltpu.matmul_acc_lhs(
                    sums[unit], rows.astype(jnp.bfloat16), load_staged_rhs=k % 2
                )
        for unit, (begin, end, column) in enumerate(shares):
            start = pl.multiple_of((step * T_BLOCK + begin) * GROUP, GROUP)
            y_ref[pl.ds(start, (end - begin) * GROUP), column : column + MXU] = (
                pltpu.matmul_pop(sums[unit])
            )

    pl.run_scoped(
        multiply,
        *[
            pltpu.ACC(unit)(((end - begin) * GROUP, MXU), jnp.float32)
            for unit, (begin, end, column) in enumerate(shares)
        ],
    )

    @pl.when(step == pl.num_programs(1) - 1)
    def _():
        part = 8

        def taps_sum(s, count):
            if halves == 1:
                total = y_ref[pl.ds(s * GROUP, count * GROUP), :LANES]
                for k in range(1, TAPS):
                    lanes = slice(k * LANES, (k + 1) * LANES)
                    total = total + y_ref[pl.ds((s + k) * GROUP, count * GROUP), lanes]
                return total
            low = y_ref[pl.ds(s * GROUP, count * GROUP), :LANES]
            return low + y_ref[pl.ds((s + 2) * GROUP, count * GROUP), LANES:]

        def combine(i, power):
            s = i * part
            size = part * GROUP
            if halves == 1:
                both = taps_sum(s, part)
            else:
                first = taps_sum(s, part + 1)
                second = taps_sum(s + depth, part + 1)
                lane = lax.broadcasted_iota(jnp.int32, (size, LANES), 1)
                low = first[:size] + pltpu.roll(first[GROUP:], width, 1)
                high = pltpu.roll(second[:size], width, 1) + second[GROUP:]
                both = jnp.where(lane < width, low, high)
            u_ref[pl.ds(pl.multiple_of(s * GROUP, size), size), :] = both
            return power + jnp.sum((both * both).reshape(part, GROUP, LANES), axis=0)

        power = lax.fori_loop(
            0, depth // part, combine, jnp.zeros((GROUP, LANES), jnp.float32)
        )
        shift = channels
        while shift < LANES:
            power = power + pltpu.roll(power, shift, 1)
            shift *= 2
        s_ref[...] = lax.rsqrt(power / S + 1e-06) * (1.0 / math.sqrt(S))

        per_half = depth // LANES
        for a in range(GROUP):
            spectra = (u_ref[pl.ds(a, depth, stride=GROUP), :] * s_ref[a : a + 1, :]).T
            for h in range(halves):
                for r in range(2):
                    first = (2 * h + r) * channels
                    for j in range(per_half):
                        z_ref[
                            r * (S // LANES) + h * per_half + j,
                            pl.ds(a, channels, stride=GROUP),
                            :,
                        ] = spectra[first : first + channels, j * LANES : (j + 1) * LANES]
        for part in range(2 * S // LANES):
            lanes = slice(part * LANES, (part + 1) * LANES)
            o_ref[:, :, lanes] = z_ref[part].astype(jnp.bfloat16).reshape(channels, GROUP, LANES)


def channelize(voltages, table, after, stream, block):
    samples = voltages.shape[1]
    columns = table.shape[1]
    channels = columns // (2 * TAPS)
    frames = samples // P_SIZE
    groups = block // GROUP
    return pl.pallas_call(
        functools.partial(channelize_kernel, channels),
        grid=(groups, frames // T_BLOCK),
        in_specs=[
            pl.BlockSpec((GROUP, T_BLOCK * P_SIZE), lambda g, t: (stream * groups + g, t)),
            pl.BlockSpec((P_SIZE, columns), lambda g, t: (0, 0)),
            pl.BlockSpec(memory_space=pl.ANY),
        ],
        out_specs=pl.BlockSpec((channels, GROUP, 2 * S), lambda g, t: (0, g, 0)),
        out_shape=jax.ShapeDtypeStruct((channels, block, 2 * S), jnp.bfloat16),
        scratch_shapes=[
            pltpu.VMEM((frames * GROUP, columns), jnp.float32),
            pltpu.VMEM((S * 2 * channels // LANES * GROUP, LANES), jnp.float32),
            pltpu.VMEM((GROUP, LANES), jnp.float32),
            pltpu.VMEM((2 * S // LANES, channels * GROUP, LANES), jnp.float32),
        ],
        compiler_params=pltpu.CompilerParams(vmem_limit_bytes=40 * 1024 * 1024),
        cost_estimate=pl.CostEstimate(
            flops=2 * block * samples * columns,
            bytes_accessed=2 * block * samples,
            transcendentals=0,
        ),
        name="channelize",
    )(voltages, table, after)


def correlate_kernel(groups, place_ref, *refs):
    o_ref, token_ref = refs[-2:]
    token_ref[...] = jnp.zeros_like(token_ref)
    own, same, other = (refs[i * groups : (i + 1) * groups] for i in range(3))
    freq_count = own[0].shape[0]
    freq, core = place_ref[0], place_ref[1]
    rows = freq_count * groups * own[0].shape[1]

    def inputs_of(sources):
        return joined([source[f ^ freq] for f in range(freq_count) for source in sources])

    left = inputs_of(own)
    turned = jnp.concatenate([left[:, S:], -left[:, :S]], axis=1)
    stacked = jnp.concatenate([left, turned], axis=0).astype(jnp.bfloat16)
    rights = [inputs_of(sources).astype(jnp.bfloat16) for sources in (same, other)]

    def keep(products, parity):
        products = products.astype(jnp.bfloat16)
        column = pl.multiple_of(parity * rows, rows)
        o_ref[0, :, pl.ds(column, rows)] = products[:rows]
        o_ref[1, :, pl.ds(column, rows)] = products[rows:]

    def multiply(*sums):
        for k in range(2 * S // MXU):
            depths = slice(k * MXU, (k + 1) * MXU)
            for unit, right in enumerate(rights):
                pltpu.matmul_push_rhs(right[:, depths], k % 2, unit, transpose=True)
            for unit in range(2):
                pltpu.matmul_acc_lhs(sums[unit], stacked[:, depths], load_staged_rhs=k % 2)
        for unit, parity in enumerate((core, 1 - core)):
            keep(pltpu.matmul_pop(sums[unit]), parity)

    if rows == MXU:
        pl.run_scoped(
            multiply, *[pltpu.ACC(unit)((2 * rows, MXU), jnp.float32) for unit in range(2)]
        )
    else:
        for right, parity in zip(rights, (core, 1 - core)):
            products = lax.dot_general(
                stacked, right, (((1,), (1,)), ((), ())), preferred_element_type=jnp.float32
            )
            keep(products, parity)


def correlate(place, own, same, other, after, previous, total_columns):
    groups = len(own)
    freq_count, slab, block, depth = own[0].shape
    rows = freq_count * groups * block
    piece = pl.BlockSpec((freq_count, None, block, depth), lambda c, p: (0, c, 0, 0))
    in_specs = [piece] * (3 * groups) + [pl.BlockSpec(memory_space=pl.ANY)]
    args = [place, *own, *same, *other, after]
    aliases = {}
    if previous is not None:
        aliases = {len(args): 0}
        in_specs.append(pl.BlockSpec(memory_space=pl.ANY))
        args.append(previous)
    return pl.pallas_call(
        functools.partial(correlate_kernel, groups),
        grid_spec=pltpu.PrefetchScalarGridSpec(
            num_scalar_prefetch=1,
            grid=(slab,),
            in_specs=in_specs,
            out_specs=[
                pl.BlockSpec((2, None, rows, 2 * rows), lambda c, p: (0, c, 0, p[2])),
                pl.BlockSpec((8, LANES), lambda c, p: (0, 0)),
            ],
        ),
        out_shape=[
            jax.ShapeDtypeStruct((2, slab, rows, total_columns), jnp.bfloat16),
            jax.ShapeDtypeStruct((8, LANES), jnp.float32),
        ],
        input_output_aliases=aliases,
        compiler_params=pltpu.CompilerParams(vmem_limit_bytes=32 * 1024 * 1024),
        cost_estimate=pl.CostEstimate(flops=0, bytes_accessed=0, transcendentals=0),
        name="correlate",
    )(*args)


def on_device(voltages, fir_taps):
    freq_count = lax.axis_size("freq")
    tm_count = lax.axis_size("tm")
    inputs_here = voltages.shape[0]
    total_columns = inputs_here * freq_count * tm_count
    streams = min(2, inputs_here // GROUP)
    block = inputs_here // streams
    ring = tm_count // 2
    tm = lax.axis_index("tm").astype(jnp.int32)
    freq = lax.axis_index("freq").astype(jnp.int32)
    swap = [(i, i ^ 1) for i in range(tm_count)]
    onward = [(i, (i + 2) % tm_count) for i in range(tm_count)]

    def behind(array, *others):
        for other in others:
            array, _ = lax.optimization_barrier((array, other))
        return array

    table = folded_table(fir_taps, freq_count)
    token = jnp.zeros((8, LANES), jnp.float32)
    own, early = [], []
    for stream in range(streams):
        if stream:
            token = behind(token, own[0])
        spectra = channelize(voltages, table, token, stream, block)
        if stream:
            early = [lax.ppermute(own[0], "tm", onward)]
        spectra = spectra.reshape(freq_count, CH_DEV, block, 2 * S)
        parts = [spectra[0]]
        for k in range(1, freq_count):
            partners = [(i, i ^ k) for i in range(freq_count)]
            parts.append(lax.ppermute(spectra[k], "freq", partners))
        if stream:
            parts[-1] = behind(parts[-1], early[0])
        own.append(jnp.stack(parts))

    result, held, tokens = None, own, []
    for step in range(ring):
        if step:
            moved = []
            for stream, piece in enumerate(held):
                if step >= 3 and streams == 2:
                    piece = behind(piece, tokens[step - 3 + stream])
                moved.append(early.pop() if early else lax.ppermute(piece, "tm", onward))
            held = moved
        other = []
        for stream, piece in enumerate(held):
            if step == ring - 1 and step and stream == streams - 1:
                piece = behind(piece, tokens[-1])
            other.append(lax.ppermute(piece, "tm", swap))
        place = jnp.stack([freq, tm % 2, (tm // 2 + ring - step) % ring])
        result, token = correlate(place, own, held, other, token, result, total_columns)
        tokens.append(token)
    return result


def solution(mesh):
    placed = (P(("tm", "freq"), None), P())
    return jax.shard_map(
        on_device,
        mesh=mesh,
        in_specs=placed,
        out_specs=P(None, "freq", "tm", None),
        check_vma=False,
    )
```

```python
import functools
import math

import jax
import jax.numpy as jnp
from jax import lax
from jax.experimental import pallas as pl
from jax.experimental.pallas import tpu as pltpu
from jax.sharding import PartitionSpec as P

P_SIZE = 2048
TAPS = 4
FIRST_BIN = 512
CH_DEV = 8
S = 256
GROUP = 16
T_BLOCK = 37
MXU = 256
SLOTS = 4
PARTS = ((0, 10), (10, 19), (19, 28), (28, 37))
CH_STEP = 2
LANES = 128


def folded_table(fir_taps, freq_count):
    slabs = jnp.arange(freq_count, dtype=jnp.int32) ^ lax.axis_index("freq").astype(jnp.int32)
    channel = slabs[:, None] * CH_DEV + jnp.arange(CH_DEV, dtype=jnp.int32)[None, :]
    bins = FIRST_BIN + channel.reshape(-1)
    points = jnp.arange(P_SIZE, dtype=jnp.int32)
    phase = points[:, None] * bins[None, :] % P_SIZE
    angle = 2.0 * math.pi / P_SIZE * phase.astype(jnp.float32)
    twiddle = jnp.concatenate([jnp.cos(angle), -jnp.sin(angle)], axis=1)
    twiddle = twiddle.astype(jnp.bfloat16).astype(jnp.float32)
    folded = fir_taps.T[:, :, None] * twiddle[:, None, :]
    return folded.reshape(P_SIZE, -1).astype(jnp.bfloat16)


def joined(pieces):
    return jnp.concatenate([piece.astype(jnp.float32) for piece in pieces], axis=0)


def unit_shares(columns):
    if columns == MXU:
        half = T_BLOCK // 2
        return [(0, half, 0), (half, T_BLOCK, 0)]
    return [(0, T_BLOCK, 0), (0, T_BLOCK, MXU)]


def channelize_kernel(
    channels, first_group, x_hbm, w_ref, after_ref, o_ref, y_ref, u_ref, s_ref, z_ref, x_ref, sems
):
    step = pl.program_id(1)
    steps = pl.num_programs(1)
    count = pl.num_programs(0) * steps
    now = pl.program_id(0) * steps + step

    def copies(block):
        slot = lax.rem(block, SLOTS)
        row = pl.multiple_of((first_group + lax.div(block, steps)) * GROUP, GROUP)
        for part, (begin, end) in enumerate(PARTS):
            lane = (lax.rem(block, steps) * T_BLOCK + begin) * P_SIZE
            start = pl.multiple_of(lane, P_SIZE)
            yield pltpu.make_async_copy(
                x_hbm.at[pl.ds(row, GROUP), pl.ds(start, (end - begin) * P_SIZE)],
                x_ref.at[slot, :, pl.ds(begin * P_SIZE, (end - begin) * P_SIZE)],
                sems.at[slot, part],
            )

    @pl.when(now == 0)
    def _():
        for block in range(SLOTS - 1):
            for copy in copies(block):
                copy.start()

    @pl.when(now + SLOTS - 1 < count)
    def _():
        for copy in copies(now + SLOTS - 1):
            copy.start()

    for copy in copies(now):
        copy.wait()
    slot = lax.rem(now, SLOTS)
    width = 2 * channels
    halves = LANES // width
    depth = S // halves
    shares = unit_shares(w_ref.shape[1])

    def multiply(*sums):
        for k in range(P_SIZE // MXU):
            depths = slice(k * MXU, (k + 1) * MXU)
            for unit, (begin, end, column) in enumerate(shares):
                pltpu.matmul_push_rhs(w_ref[depths, column : column + MXU], k % 2, unit)
            for unit, (begin, end, column) in enumerate(shares):
                rows = joined(
                    [
                        x_ref[slot, :, t * P_SIZE + k * MXU : t * P_SIZE + (k + 1) * MXU]
                        for t in range(begin, end)
                    ]
                )
                pltpu.matmul_acc_lhs(
                    sums[unit], rows.astype(jnp.bfloat16), load_staged_rhs=k % 2
                )
        for unit, (begin, end, column) in enumerate(shares):
            start = pl.multiple_of((step * T_BLOCK + begin) * GROUP, GROUP)
            y_ref[pl.ds(start, (end - begin) * GROUP), column : column + MXU] = (
                pltpu.matmul_pop(sums[unit])
            )

    pl.run_scoped(
        multiply,
        *[
            pltpu.ACC(unit)(((end - begin) * GROUP, MXU), jnp.float32)
            for unit, (begin, end, column) in enumerate(shares)
        ],
    )

    @pl.when(step == steps - 1)
    def _():
        part = 8

        def taps_sum(s, count):
            if halves == 1:
                total = y_ref[pl.ds(s * GROUP, count * GROUP), :LANES]
                for k in range(1, TAPS):
                    lanes = slice(k * LANES, (k + 1) * LANES)
                    total = total + y_ref[pl.ds((s + k) * GROUP, count * GROUP), lanes]
                return total
            low = y_ref[pl.ds(s * GROUP, count * GROUP), :LANES]
            return low + y_ref[pl.ds((s + 2) * GROUP, count * GROUP), LANES:]

        def combine(i, power):
            s = i * part
            size = part * GROUP
            if halves == 1:
                both = taps_sum(s, part)
            else:
                first = taps_sum(s, part + 1)
                second = taps_sum(s + depth, part + 1)
                lane = lax.broadcasted_iota(jnp.int32, (size, LANES), 1)
                low = first[:size] + pltpu.roll(first[GROUP:], width, 1)
                high = pltpu.roll(second[:size], width, 1) + second[GROUP:]
                both = jnp.where(lane < width, low, high)
            u_ref[pl.ds(pl.multiple_of(s * GROUP, size), size), :] = both
            return power + jnp.sum((both * both).reshape(part, GROUP, LANES), axis=0)

        power = lax.fori_loop(
            0, depth // part, combine, jnp.zeros((GROUP, LANES), jnp.float32)
        )
        shift = channels
        while shift < LANES:
            power = power + pltpu.roll(power, shift, 1)
            shift *= 2
        s_ref[...] = lax.rsqrt(power / S + 1e-06) * (1.0 / math.sqrt(S))

        per_half = depth // LANES
        for a in range(GROUP):
            spectra = (u_ref[pl.ds(a, depth, stride=GROUP), :] * s_ref[a : a + 1, :]).T
            for h in range(halves):
                for r in range(2):
                    first = (2 * h + r) * channels
                    for j in range(per_half):
                        z_ref[
                            r * (S // LANES) + h * per_half + j,
                            pl.ds(a, channels, stride=GROUP),
                            :,
                        ] = spectra[first : first + channels, j * LANES : (j + 1) * LANES]
        for part in range(2 * S // LANES):
            lanes = slice(part * LANES, (part + 1) * LANES)
            o_ref[:, :, lanes] = z_ref[part].astype(jnp.bfloat16).reshape(channels, GROUP, LANES)


def channelize(voltages, table, after, first_group, groups):
    samples = voltages.shape[1]
    columns = table.shape[1]
    channels = columns // (2 * TAPS)
    frames = samples // P_SIZE
    return pl.pallas_call(
        functools.partial(channelize_kernel, channels, first_group),
        grid=(groups, frames // T_BLOCK),
        in_specs=[
            pl.BlockSpec(memory_space=pl.ANY),
            pl.BlockSpec((P_SIZE, columns), lambda g, t: (0, 0)),
            pl.BlockSpec(memory_space=pl.ANY),
        ],
        out_specs=pl.BlockSpec((channels, GROUP, 2 * S), lambda g, t: (0, g, 0)),
        out_shape=jax.ShapeDtypeStruct((channels, groups * GROUP, 2 * S), jnp.bfloat16),
        scratch_shapes=[
            pltpu.VMEM((frames * GROUP, columns), jnp.float32),
            pltpu.VMEM((S * 2 * channels // LANES * GROUP, LANES), jnp.float32),
            pltpu.VMEM((GROUP, LANES), jnp.float32),
            pltpu.VMEM((2 * S // LANES, channels * GROUP, LANES), jnp.float32),
            pltpu.VMEM((SLOTS, GROUP, T_BLOCK * P_SIZE), jnp.bfloat16),
            pltpu.SemaphoreType.DMA((SLOTS, len(PARTS))),
        ],
        compiler_params=pltpu.CompilerParams(vmem_limit_bytes=40 * 1024 * 1024),
        cost_estimate=pl.CostEstimate(
            flops=2 * groups * GROUP * samples * columns,
            bytes_accessed=2 * groups * GROUP * samples,
            transcendentals=0,
        ),
        name="channelize",
    )(voltages, table, after)


def correlate_kernel(streams, place_ref, *refs):
    o_ref, token_ref = refs[-2:]
    token_ref[...] = jnp.zeros_like(token_ref)
    own, same, other = (refs[i * streams : (i + 1) * streams] for i in range(3))
    freq_count, channels = own[0].shape[1:3]
    freq, core = place_ref[0], place_ref[1]
    rows = freq_count * sum(piece.shape[0] * piece.shape[3] for piece in own)

    def inputs_of(sources, channel):
        pieces = [
            source[g, f ^ freq, channel]
            for f in range(freq_count)
            for source in sources
            for g in range(source.shape[0])
        ]
        return joined(pieces)

    def one_channel(channel):
        left = inputs_of(own, channel)
        turned = jnp.concatenate([left[:, S:], -left[:, :S]], axis=1)
        stacked = jnp.concatenate([left, turned], axis=0).astype(jnp.bfloat16)
        rights = [inputs_of(sources, channel).astype(jnp.bfloat16) for sources in (same, other)]

        def keep(products, parity):
            products = products.astype(jnp.bfloat16)
            column = pl.multiple_of(parity * rows, rows)
            o_ref[0, channel, :, pl.ds(column, rows)] = products[:rows]
            o_ref[1, channel, :, pl.ds(column, rows)] = products[rows:]

        def multiply(*sums):
            for k in range(2 * S // MXU):
                depths = slice(k * MXU, (k + 1) * MXU)
                for unit, right in enumerate(rights):
                    pltpu.matmul_push_rhs(right[:, depths], k % 2, unit, transpose=True)
                for unit in range(2):
                    pltpu.matmul_acc_lhs(sums[unit], stacked[:, depths], load_staged_rhs=k % 2)
            for unit, parity in enumerate((core, 1 - core)):
                keep(pltpu.matmul_pop(sums[unit]), parity)

        if rows == MXU:
            pl.run_scoped(
                multiply, *[pltpu.ACC(unit)((2 * rows, MXU), jnp.float32) for unit in range(2)]
            )
        else:
            for right, parity in zip(rights, (core, 1 - core)):
                products = lax.dot_general(
                    stacked, right, (((1,), (1,)), ((), ())), preferred_element_type=jnp.float32
                )
                keep(products, parity)

    for channel in range(channels):
        one_channel(channel)


def correlate(place, own, same, other, after, previous, total_columns):
    streams = len(own)
    freq_count, slab, _, depth = own[0].shape[1:]
    rows = freq_count * sum(piece.shape[0] * piece.shape[3] for piece in own)
    in_specs = [
        pl.BlockSpec(
            (piece.shape[0], freq_count, CH_STEP, piece.shape[3], depth),
            lambda c, p: (0, 0, c, 0, 0),
        )
        for piece in (*own, *same, *other)
    ]
    in_specs.append(pl.BlockSpec(memory_space=pl.ANY))
    args = [place, *own, *same, *other, after]
    aliases = {}
    if previous is not None:
        aliases = {len(args): 0}
        in_specs.append(pl.BlockSpec(memory_space=pl.ANY))
        args.append(previous)
    return pl.pallas_call(
        functools.partial(correlate_kernel, streams),
        grid_spec=pltpu.PrefetchScalarGridSpec(
            num_scalar_prefetch=1,
            grid=(slab // CH_STEP,),
            in_specs=in_specs,
            out_specs=[
                pl.BlockSpec((2, CH_STEP, rows, 2 * rows), lambda c, p: (0, c, 0, p[2])),
                pl.BlockSpec((8, LANES), lambda c, p: (0, 0)),
            ],
        ),
        out_shape=[
            jax.ShapeDtypeStruct((2, slab, rows, total_columns), jnp.bfloat16),
            jax.ShapeDtypeStruct((8, LANES), jnp.float32),
        ],
        input_output_aliases=aliases,
        compiler_params=pltpu.CompilerParams(vmem_limit_bytes=32 * 1024 * 1024),
        cost_estimate=pl.CostEstimate(flops=0, bytes_accessed=0, transcendentals=0),
        name="correlate",
    )(*args)


def on_device(voltages, fir_taps):
    freq_count = lax.axis_size("freq")
    tm_count = lax.axis_size("tm")
    inputs_here = voltages.shape[0]
    total_columns = inputs_here * freq_count * tm_count
    groups = inputs_here // GROUP
    streams = min(2, groups)
    ring = tm_count // 2
    tm = lax.axis_index("tm").astype(jnp.int32)
    freq = lax.axis_index("freq").astype(jnp.int32)
    swap = [(i, i ^ 1) for i in range(tm_count)]
    onward = [(i, (i + 2) % tm_count) for i in range(tm_count)]

    def behind(array, *others):
        for other in others:
            array, _ = lax.optimization_barrier((array, other))
        return array

    table = folded_table(fir_taps, freq_count)
    token = jnp.zeros((8, LANES), jnp.float32)
    own, early = [], []
    for stream in range(streams):
        first, last = stream * groups // streams, (stream + 1) * groups // streams
        at_once = 1 if stream == 0 else last - first
        if stream:
            token = behind(token, own[0])
        parts = []
        for group in range(first, last, at_once):
            spectra = channelize(voltages, table, token, group, at_once)
            token = behind(token, spectra)
            spectra = spectra.reshape(freq_count, CH_DEV, at_once * GROUP, 2 * S)
            parts.append(spectra[0])
            for k in range(1, freq_count):
                partners = [(i, i ^ k) for i in range(freq_count)]
                parts.append(lax.ppermute(spectra[k], "freq", partners))
        if stream:
            early = [lax.ppermute(own[0], "tm", onward)]
            parts[-1] = behind(parts[-1], early[0])
        own.append(jnp.stack(parts).reshape(-1, freq_count, *parts[0].shape))

    result, held, tokens = None, own, []
    for step in range(ring):
        if step:
            moved = []
            for stream, piece in enumerate(held):
                if step >= 3 and streams == 2:
                    piece = behind(piece, tokens[step - 3 + stream])
                moved.append(early.pop() if early else lax.ppermute(piece, "tm", onward))
            held = moved
        other = []
        for stream, piece in enumerate(held):
            if step == ring - 1 and step and stream == streams - 1:
                piece = behind(piece, tokens[-1])
            other.append(lax.ppermute(piece, "tm", swap))
        place = jnp.stack([freq, tm % 2, (tm // 2 + ring - step) % ring])
        result, token = correlate(place, own, held, other, token, result, total_columns)
        tokens.append(token)
    return result


def solution(mesh):
    placed = (P(("tm", "freq"), None), P())
    return jax.shard_map(
        on_device,
        mesh=mesh,
        in_specs=placed,
        out_specs=P(None, "freq", "tm", None),
        check_vma=False,
    )
```

```python
import functools
import math

import jax
import jax.numpy as jnp
from jax import lax
from jax.experimental import pallas as pl
from jax.experimental.pallas import tpu as pltpu
from jax.sharding import PartitionSpec as P

P_SIZE = 2048
TAPS = 4
FIRST_BIN = 512
CH_DEV = 8
S = 256
GROUP = 16
T_BLOCK = 37
MXU = 256
SLOTS = 4
PARTS = ((0, 10), (10, 19), (19, 28), (28, 37))
CH_STEP = 2
LANES = 128


def folded_table(fir_taps, freq_count):
    slabs = jnp.arange(freq_count, dtype=jnp.int32) ^ lax.axis_index("freq").astype(jnp.int32)
    channel = slabs[:, None] * CH_DEV + jnp.arange(CH_DEV, dtype=jnp.int32)[None, :]
    bins = FIRST_BIN + channel.reshape(-1)
    points = jnp.arange(P_SIZE, dtype=jnp.int32)
    phase = points[:, None] * bins[None, :] % P_SIZE
    angle = 2.0 * math.pi / P_SIZE * phase.astype(jnp.float32)
    twiddle = jnp.concatenate([jnp.cos(angle), -jnp.sin(angle)], axis=1)
    twiddle = twiddle.astype(jnp.bfloat16).astype(jnp.float32)
    folded = fir_taps.T[:, :, None] * twiddle[:, None, :]
    return folded.reshape(P_SIZE, -1).astype(jnp.bfloat16)


def joined(pieces):
    return jnp.concatenate([piece.astype(jnp.float32) for piece in pieces], axis=0)


def unit_shares(columns):
    if columns == MXU:
        half = T_BLOCK // 2
        return [(0, half, 0), (half, T_BLOCK, 0)]
    return [(0, T_BLOCK, 0), (0, T_BLOCK, MXU)]


def channelize_kernel(
    channels, first_group, x_hbm, w_ref, after_ref, o_ref, y_ref, u_ref, s_ref, z_ref, x_ref, sems
):
    step = pl.program_id(1)
    steps = pl.num_programs(1)
    count = pl.num_programs(0) * steps
    now = pl.program_id(0) * steps + step

    def copies(block):
        slot = lax.rem(block, SLOTS)
        row = pl.multiple_of((first_group + lax.div(block, steps)) * GROUP, GROUP)
        for part, (begin, end) in enumerate(PARTS):
            lane = (lax.rem(block, steps) * T_BLOCK + begin) * P_SIZE
            start = pl.multiple_of(lane, P_SIZE)
            yield pltpu.make_async_copy(
                x_hbm.at[pl.ds(row, GROUP), pl.ds(start, (end - begin) * P_SIZE)],
                x_ref.at[slot, :, pl.ds(begin * P_SIZE, (end - begin) * P_SIZE)],
                sems.at[slot, part],
            )

    @pl.when(now == 0)
    def _():
        for block in range(SLOTS - 1):
            for copy in copies(block):
                copy.start()

    @pl.when(now + SLOTS - 1 < count)
    def _():
        for copy in copies(now + SLOTS - 1):
            copy.start()

    for copy in copies(now):
        copy.wait()
    slot = lax.rem(now, SLOTS)
    width = 2 * channels
    halves = LANES // width
    depth = S // halves
    shares = unit_shares(w_ref.shape[1])

    def multiply(*sums):
        for k in range(P_SIZE // MXU):
            depths = slice(k * MXU, (k + 1) * MXU)
            for unit, (begin, end, column) in enumerate(shares):
                pltpu.matmul_push_rhs(w_ref[depths, column : column + MXU], k % 2, unit)
            for unit, (begin, end, column) in enumerate(shares):
                rows = jnp.concatenate(
                    [
                        x_ref[slot, :, t * P_SIZE + k * MXU : t * P_SIZE + (k + 1) * MXU]
                        for t in range(begin, end)
                    ],
                    axis=0,
                )
                pltpu.matmul_acc_lhs(sums[unit], rows, load_staged_rhs=k % 2)
        for unit, (begin, end, column) in enumerate(shares):
            start = pl.multiple_of((step * T_BLOCK + begin) * GROUP, GROUP)
            y_ref[pl.ds(start, (end - begin) * GROUP), column : column + MXU] = (
                pltpu.matmul_pop(sums[unit])
            )

    pl.run_scoped(
        multiply,
        *[
            pltpu.ACC(unit)(((end - begin) * GROUP, MXU), jnp.float32)
            for unit, (begin, end, column) in enumerate(shares)
        ],
    )

    @pl.when(step == steps - 1)
    def _():
        part = 8

        def taps_sum(s, count):
            if halves == 1:
                total = y_ref[pl.ds(s * GROUP, count * GROUP), :LANES]
                for k in range(1, TAPS):
                    lanes = slice(k * LANES, (k + 1) * LANES)
                    total = total + y_ref[pl.ds((s + k) * GROUP, count * GROUP), lanes]
                return total
            low = y_ref[pl.ds(s * GROUP, count * GROUP), :LANES]
            return low + y_ref[pl.ds((s + 2) * GROUP, count * GROUP), LANES:]

        def combine(i, power):
            s = i * part
            size = part * GROUP
            if halves == 1:
                both = taps_sum(s, part)
            else:
                first = taps_sum(s, part + 1)
                second = taps_sum(s + depth, part + 1)
                lane = lax.broadcasted_iota(jnp.int32, (size, LANES), 1)
                low = first[:size] + pltpu.roll(first[GROUP:], width, 1)
                high = pltpu.roll(second[:size], width, 1) + second[GROUP:]
                both = jnp.where(lane < width, low, high)
            u_ref[pl.ds(pl.multiple_of(s * GROUP, size), size), :] = both
            return power + jnp.sum((both * both).reshape(part, GROUP, LANES), axis=0)

        power = lax.fori_loop(
            0, depth // part, combine, jnp.zeros((GROUP, LANES), jnp.float32)
        )
        shift = channels
        while shift < LANES:
            power = power + pltpu.roll(power, shift, 1)
            shift *= 2
        s_ref[...] = lax.rsqrt(power / S + 1e-06) * (1.0 / math.sqrt(S))

        per_half = depth // LANES
        for a in range(GROUP):
            spectra = (u_ref[pl.ds(a, depth, stride=GROUP), :] * s_ref[a : a + 1, :]).T
            for h in range(halves):
                for r in range(2):
                    first = (2 * h + r) * channels
                    for j in range(per_half):
                        z_ref[
                            r * (S // LANES) + h * per_half + j,
                            pl.ds(a, channels, stride=GROUP),
                            :,
                        ] = spectra[first : first + channels, j * LANES : (j + 1) * LANES]
        for part in range(2 * S // LANES):
            lanes = slice(part * LANES, (part + 1) * LANES)
            o_ref[:, :, lanes] = z_ref[part].astype(jnp.bfloat16).reshape(channels, GROUP, LANES)


def channelize(voltages, table, after, first_group, groups):
    samples = voltages.shape[1]
    columns = table.shape[1]
    channels = columns // (2 * TAPS)
    frames = samples // P_SIZE
    return pl.pallas_call(
        functools.partial(channelize_kernel, channels, first_group),
        grid=(groups, frames // T_BLOCK),
        in_specs=[
            pl.BlockSpec(memory_space=pl.ANY),
            pl.BlockSpec((P_SIZE, columns), lambda g, t: (0, 0)),
            pl.BlockSpec(memory_space=pl.ANY),
        ],
        out_specs=pl.BlockSpec((channels, GROUP, 2 * S), lambda g, t: (0, g, 0)),
        out_shape=jax.ShapeDtypeStruct((channels, groups * GROUP, 2 * S), jnp.bfloat16),
        scratch_shapes=[
            pltpu.VMEM((frames * GROUP, columns), jnp.float32),
            pltpu.VMEM((S * 2 * channels // LANES * GROUP, LANES), jnp.float32),
            pltpu.VMEM((GROUP, LANES), jnp.float32),
            pltpu.VMEM((2 * S // LANES, channels * GROUP, LANES), jnp.float32),
            pltpu.VMEM((SLOTS, GROUP, T_BLOCK * P_SIZE), jnp.bfloat16),
            pltpu.SemaphoreType.DMA((SLOTS, len(PARTS))),
        ],
        compiler_params=pltpu.CompilerParams(vmem_limit_bytes=40 * 1024 * 1024),
        cost_estimate=pl.CostEstimate(
            flops=2 * groups * GROUP * samples * columns,
            bytes_accessed=2 * groups * GROUP * samples,
            transcendentals=0,
        ),
        name="channelize",
    )(voltages, table, after)


def correlate_kernel(counts, place_ref, *refs):
    o_ref, token_ref = refs[-2:]
    token_ref[...] = jnp.zeros_like(token_ref)
    own, same, other = (refs[sum(counts[:i]) : sum(counts[: i + 1])] for i in range(3))
    freq_count, channels = own[0].shape[:2]
    freq, core = place_ref[0], place_ref[1]
    rows = freq_count * sum(piece.shape[2] for piece in own)

    def inputs_of(sources, channel):
        return joined([source[f ^ freq, channel] for f in range(freq_count) for source in sources])

    def one_channel(channel):
        left = inputs_of(own, channel)
        turned = jnp.concatenate([left[:, S:], -left[:, :S]], axis=1)
        stacked = jnp.concatenate([left, turned], axis=0).astype(jnp.bfloat16)
        rights = [inputs_of(sources, channel).astype(jnp.bfloat16) for sources in (same, other)]

        def keep(products, parity):
            products = products.astype(jnp.bfloat16)
            column = pl.multiple_of(parity * rows, rows)
            o_ref[0, channel, :, pl.ds(column, rows)] = products[:rows]
            o_ref[1, channel, :, pl.ds(column, rows)] = products[rows:]

        def multiply(*sums):
            for k in range(2 * S // MXU):
                depths = slice(k * MXU, (k + 1) * MXU)
                for unit, right in enumerate(rights):
                    pltpu.matmul_push_rhs(right[:, depths], k % 2, unit, transpose=True)
                for unit in range(2):
                    pltpu.matmul_acc_lhs(sums[unit], stacked[:, depths], load_staged_rhs=k % 2)
            for unit, parity in enumerate((core, 1 - core)):
                keep(pltpu.matmul_pop(sums[unit]), parity)

        if rows == MXU:
            pl.run_scoped(
                multiply, *[pltpu.ACC(unit)((2 * rows, MXU), jnp.float32) for unit in range(2)]
            )
        else:
            for right, parity in zip(rights, (core, 1 - core)):
                products = lax.dot_general(
                    stacked, right, (((1,), (1,)), ((), ())), preferred_element_type=jnp.float32
                )
                keep(products, parity)

    for channel in range(channels):
        one_channel(channel)


def correlate(place, own, same, other, after, previous, total_columns):
    pieces = (*own, *same, *other)
    freq_count, slab, _, depth = own[0][0].shape[1:]
    rows = freq_count * sum(array.shape[3] for array, part in own)
    in_specs = [
        pl.BlockSpec(
            (None, freq_count, CH_STEP, array.shape[3], depth),
            lambda c, p, part=part: (part, 0, c, 0, 0),
        )
        for array, part in pieces
    ]
    in_specs.append(pl.BlockSpec(memory_space=pl.ANY))
    args = [place, *[array for array, part in pieces], after]
    aliases = {}
    if previous is not None:
        aliases = {len(args): 0}
        in_specs.append(pl.BlockSpec(memory_space=pl.ANY))
        args.append(previous)
    return pl.pallas_call(
        functools.partial(correlate_kernel, (len(own), len(same), len(other))),
        grid_spec=pltpu.PrefetchScalarGridSpec(
            num_scalar_prefetch=1,
            grid=(slab // CH_STEP,),
            in_specs=in_specs,
            out_specs=[
                pl.BlockSpec((2, CH_STEP, rows, 2 * rows), lambda c, p: (0, c, 0, p[2])),
                pl.BlockSpec((8, LANES), lambda c, p: (0, 0)),
            ],
        ),
        out_shape=[
            jax.ShapeDtypeStruct((2, slab, rows, total_columns), jnp.bfloat16),
            jax.ShapeDtypeStruct((8, LANES), jnp.float32),
        ],
        input_output_aliases=aliases,
        compiler_params=pltpu.CompilerParams(vmem_limit_bytes=32 * 1024 * 1024),
        cost_estimate=pl.CostEstimate(flops=0, bytes_accessed=0, transcendentals=0),
        name="correlate",
    )(*args)


def on_device(voltages, fir_taps):
    freq_count = lax.axis_size("freq")
    tm_count = lax.axis_size("tm")
    inputs_here = voltages.shape[0]
    total_columns = inputs_here * freq_count * tm_count
    groups = inputs_here // GROUP
    widths = (1, 1, groups - 2) if groups >= 3 else (1,) * groups
    streams = len(widths)
    ring = tm_count // 2
    tm = lax.axis_index("tm").astype(jnp.int32)
    freq = lax.axis_index("freq").astype(jnp.int32)
    swap = [(i, i ^ 1) for i in range(tm_count)]
    onward = [(i, (i + 2) % tm_count) for i in range(tm_count)]

    def behind(array, *others):
        for other in others:
            array, _ = lax.optimization_barrier((array, other))
        return array

    table = folded_table(fir_taps, freq_count)
    token = jnp.zeros((8, LANES), jnp.float32)
    held, swapped = {}, {}

    def move_on(step, stream, *others):
        if (step, stream) not in held:
            array, part = held[step - 1, stream]
            piece = behind(array[part : part + 1], *others)
            held[step, stream] = (lax.ppermute(piece, "tm", onward), 0)
        return held[step, stream][0]

    def swap_cores(step, stream, *others):
        array, part = held[step, stream]
        if (step, stream) not in swapped:
            for place, (other, number) in held.items():
                if other is array and place in swapped:
                    swapped[step, stream] = (swapped[place][0], part)
        if (step, stream) not in swapped:
            swapped[step, stream] = (lax.ppermute(behind(array, *others), "tm", swap), part)

    ahead = streams == 3 and ring == 4
    first = 0
    for stream, width in enumerate(widths):
        if stream >= 2:
            token = behind(token, *[held[0, earlier][0] for earlier in range(stream)])
        spectra = channelize(voltages, table, token, first, width)
        first += width
        token = behind(token, spectra)
        spectra = spectra.reshape(freq_count, CH_DEV, width * GROUP, 2 * S)
        parts = [spectra[0]]
        for k in range(1, freq_count):
            partners = [(i, i ^ k) for i in range(freq_count)]
            parts.append(lax.ppermute(spectra[k], "freq", partners))
        if ahead and stream == 2:
            parts[-1] = behind(parts[-1], move_on(1, 1), move_on(1, 0), move_on(2, 0))
        held[0, stream] = (jnp.stack(parts)[None], 0)

    if ahead:
        both = jnp.concatenate([held[2, 0][0], held[1, 1][0]], axis=0)
        both = lax.ppermute(both, "tm", onward)
        held[3, 0], held[2, 1] = (both, 0), (both, 1)
    names = list(range(streams))
    result, tokens = None, [token]
    for step in range(ring):
        if ahead and step == 2:
            third, names = held[1, 2][0], [0, 1, 2, 3]
            middle = third.shape[3] // 2
            held[1, 2], held[1, 3] = (third[:, :, :, :middle], 0), (third[:, :, :, middle:], 0)
        for name in names:
            if step:
                late = ahead and step == 3 and name == 3
                move_on(step, name, *([tokens[2]] if late else []))
        for name in names:
            late = step == ring - 1 and step and name == names[-1]
            swap_cores(step, name, *([tokens[-1]] if late else []))
        place = jnp.stack([freq, tm % 2, (tm // 2 + ring - step) % ring])
        result, token = correlate(
            place,
            [held[0, name] for name in range(streams)],
            [held[step, name] for name in names],
            [swapped[step, name] for name in names],
            tokens[-1],
            result,
            total_columns,
        )
        tokens.append(token)
    return result


def solution(mesh):
    placed = (P(("tm", "freq"), None), P())
    return jax.shard_map(
        on_device,
        mesh=mesh,
        in_specs=placed,
        out_specs=P(None, "freq", "tm", None),
        check_vma=False,
    )
```

```python
import functools
import math

import jax
import jax.numpy as jnp
from jax import lax
from jax.experimental import pallas as pl
from jax.experimental.pallas import tpu as pltpu
from jax.sharding import PartitionSpec as P

P_SIZE = 2048
TAPS = 4
FIRST_BIN = 512
CH_DEV = 8
S = 256
GROUP = 16
T_BLOCK = 37
MXU = 256
SLOTS = 4
PARTS = ((0, 10), (10, 19), (19, 28), (28, 37))
CH_STEP = 2
LANES = 128


def folded_table(fir_taps, freq_count):
    slabs = jnp.arange(freq_count, dtype=jnp.int32) ^ lax.axis_index("freq").astype(jnp.int32)
    channel = slabs[:, None] * CH_DEV + jnp.arange(CH_DEV, dtype=jnp.int32)[None, :]
    bins = FIRST_BIN + channel.reshape(-1)
    points = jnp.arange(P_SIZE, dtype=jnp.int32)
    phase = points[:, None] * bins[None, :] % P_SIZE
    angle = 2.0 * math.pi / P_SIZE * phase.astype(jnp.float32)
    twiddle = jnp.concatenate([jnp.cos(angle), -jnp.sin(angle)], axis=1)
    twiddle = twiddle.astype(jnp.bfloat16).astype(jnp.float32)
    folded = fir_taps.T[:, :, None] * twiddle[:, None, :]
    return folded.reshape(P_SIZE, -1).astype(jnp.bfloat16)


def joined(pieces):
    return jnp.concatenate([piece.astype(jnp.float32) for piece in pieces], axis=0)


def unit_shares(columns):
    if columns == MXU:
        half = T_BLOCK // 2
        return [(0, half, 0), (half, T_BLOCK, 0)]
    return [(0, T_BLOCK, 0), (0, T_BLOCK, MXU)]


def channelize_kernel(
    channels, first_group, x_hbm, w_ref, after_ref, o_ref, y_ref, u_ref, s_ref, z_ref, x_ref, sems
):
    step = pl.program_id(1)
    steps = pl.num_programs(1)
    count = pl.num_programs(0) * steps
    now = pl.program_id(0) * steps + step

    def copies(block):
        slot = lax.rem(block, SLOTS)
        row = pl.multiple_of((first_group + lax.div(block, steps)) * GROUP, GROUP)
        for part, (begin, end) in enumerate(PARTS):
            lane = (lax.rem(block, steps) * T_BLOCK + begin) * P_SIZE
            start = pl.multiple_of(lane, P_SIZE)
            yield pltpu.make_async_copy(
                x_hbm.at[pl.ds(row, GROUP), pl.ds(start, (end - begin) * P_SIZE)],
                x_ref.at[slot, :, pl.ds(begin * P_SIZE, (end - begin) * P_SIZE)],
                sems.at[slot, part],
            )

    @pl.when(now == 0)
    def _():
        for block in range(SLOTS - 1):
            for copy in copies(block):
                copy.start()

    @pl.when(now + SLOTS - 1 < count)
    def _():
        for copy in copies(now + SLOTS - 1):
            copy.start()

    for copy in copies(now):
        copy.wait()
    slot = lax.rem(now, SLOTS)
    width = 2 * channels
    halves = LANES // width
    depth = S // halves
    shares = unit_shares(w_ref.shape[1])

    def multiply(*sums):
        for k in range(P_SIZE // MXU):
            depths = slice(k * MXU, (k + 1) * MXU)
            for unit, (begin, end, column) in enumerate(shares):
                pltpu.matmul_push_rhs(w_ref[depths, column : column + MXU], k % 2, unit)
            for unit, (begin, end, column) in enumerate(shares):
                rows = jnp.concatenate(
                    [
                        x_ref[slot, :, t * P_SIZE + k * MXU : t * P_SIZE + (k + 1) * MXU]
                        for t in range(begin, end)
                    ],
                    axis=0,
                )
                pltpu.matmul_acc_lhs(sums[unit], rows, load_staged_rhs=k % 2)
        for unit, (begin, end, column) in enumerate(shares):
            start = pl.multiple_of((step * T_BLOCK + begin) * GROUP, GROUP)
            y_ref[pl.ds(start, (end - begin) * GROUP), column : column + MXU] = (
                pltpu.matmul_pop(sums[unit])
            )

    pl.run_scoped(
        multiply,
        *[
            pltpu.ACC(unit)(((end - begin) * GROUP, MXU), jnp.float32)
            for unit, (begin, end, column) in enumerate(shares)
        ],
    )

    @pl.when(step == steps - 1)
    def _():
        part = 8

        def taps_sum(s, count):
            if halves == 1:
                total = y_ref[pl.ds(s * GROUP, count * GROUP), :LANES]
                for k in range(1, TAPS):
                    lanes = slice(k * LANES, (k + 1) * LANES)
                    total = total + y_ref[pl.ds((s + k) * GROUP, count * GROUP), lanes]
                return total
            low = y_ref[pl.ds(s * GROUP, count * GROUP), :LANES]
            return low + y_ref[pl.ds((s + 2) * GROUP, count * GROUP), LANES:]

        def combine(i, power):
            s = i * part
            size = part * GROUP
            if halves == 1:
                both = taps_sum(s, part)
            else:
                first = taps_sum(s, part + 1)
                second = taps_sum(s + depth, part + 1)
                lane = lax.broadcasted_iota(jnp.int32, (size, LANES), 1)
                low = first[:size] + pltpu.roll(first[GROUP:], width, 1)
                high = pltpu.roll(second[:size], width, 1) + second[GROUP:]
                both = jnp.where(lane < width, low, high)
            u_ref[pl.ds(pl.multiple_of(s * GROUP, size), size), :] = both
            return power + jnp.sum((both * both).reshape(part, GROUP, LANES), axis=0)

        power = lax.fori_loop(
            0, depth // part, combine, jnp.zeros((GROUP, LANES), jnp.float32)
        )
        shift = channels
        while shift < LANES:
            power = power + pltpu.roll(power, shift, 1)
            shift *= 2
        s_ref[...] = lax.rsqrt(power / S + 1e-06) * (1.0 / math.sqrt(S))

        per_half = depth // LANES
        for a in range(GROUP):
            spectra = (u_ref[pl.ds(a, depth, stride=GROUP), :] * s_ref[a : a + 1, :]).T
            for h in range(halves):
                for r in range(2):
                    first = (2 * h + r) * channels
                    for j in range(per_half):
                        z_ref[
                            r * (S // LANES) + h * per_half + j,
                            pl.ds(a, channels, stride=GROUP),
                            :,
                        ] = spectra[first : first + channels, j * LANES : (j + 1) * LANES]
        for part in range(2 * S // LANES):
            lanes = slice(part * LANES, (part + 1) * LANES)
            o_ref[:, :, lanes] = z_ref[part].astype(jnp.bfloat16).reshape(channels, GROUP, LANES)


def channelize(voltages, table, after, first_group, groups):
    samples = voltages.shape[1]
    columns = table.shape[1]
    channels = columns // (2 * TAPS)
    frames = samples // P_SIZE
    return pl.pallas_call(
        functools.partial(channelize_kernel, channels, first_group),
        grid=(groups, frames // T_BLOCK),
        in_specs=[
            pl.BlockSpec(memory_space=pl.ANY),
            pl.BlockSpec((P_SIZE, columns), lambda g, t: (0, 0)),
            pl.BlockSpec(memory_space=pl.ANY),
        ],
        out_specs=pl.BlockSpec((channels, GROUP, 2 * S), lambda g, t: (0, g, 0)),
        out_shape=jax.ShapeDtypeStruct((channels, groups * GROUP, 2 * S), jnp.bfloat16),
        scratch_shapes=[
            pltpu.VMEM((frames * GROUP, columns), jnp.float32),
            pltpu.VMEM((S * 2 * channels // LANES * GROUP, LANES), jnp.float32),
            pltpu.VMEM((GROUP, LANES), jnp.float32),
            pltpu.VMEM((2 * S // LANES, channels * GROUP, LANES), jnp.float32),
            pltpu.VMEM((SLOTS, GROUP, T_BLOCK * P_SIZE), jnp.bfloat16),
            pltpu.SemaphoreType.DMA((SLOTS, len(PARTS))),
        ],
        compiler_params=pltpu.CompilerParams(vmem_limit_bytes=40 * 1024 * 1024),
        cost_estimate=pl.CostEstimate(
            flops=2 * groups * GROUP * samples * columns,
            bytes_accessed=2 * groups * GROUP * samples,
            transcendentals=0,
        ),
        name="channelize",
    )(voltages, table, after)


def correlate_kernel(counts, place_ref, *refs):
    o_ref, token_ref = refs[-2:]
    token_ref[...] = jnp.zeros_like(token_ref)
    own, same, other = (refs[sum(counts[:i]) : sum(counts[: i + 1])] for i in range(3))
    freq_count, channels = own[0].shape[:2]
    freq, core = place_ref[0], place_ref[1]
    rows = freq_count * sum(piece.shape[2] for piece in own)

    def inputs_of(sources, channel):
        return joined([source[f ^ freq, channel] for f in range(freq_count) for source in sources])

    def one_channel(channel):
        left = inputs_of(own, channel)
        turned = jnp.concatenate([left[:, S:], -left[:, :S]], axis=1)
        stacked = jnp.concatenate([left, turned], axis=0).astype(jnp.bfloat16)
        rights = [inputs_of(sources, channel).astype(jnp.bfloat16) for sources in (same, other)]

        def keep(products, parity):
            products = products.astype(jnp.bfloat16)
            column = pl.multiple_of(parity * rows, rows)
            o_ref[0, channel, :, pl.ds(column, rows)] = products[:rows]
            o_ref[1, channel, :, pl.ds(column, rows)] = products[rows:]

        def multiply(*sums):
            for k in range(2 * S // MXU):
                depths = slice(k * MXU, (k + 1) * MXU)
                for unit, right in enumerate(rights):
                    pltpu.matmul_push_rhs(right[:, depths], k % 2, unit, transpose=True)
                for unit in range(2):
                    pltpu.matmul_acc_lhs(sums[unit], stacked[:, depths], load_staged_rhs=k % 2)
            for unit, parity in enumerate((core, 1 - core)):
                keep(pltpu.matmul_pop(sums[unit]), parity)

        if rows == MXU:
            pl.run_scoped(
                multiply, *[pltpu.ACC(unit)((2 * rows, MXU), jnp.float32) for unit in range(2)]
            )
        else:
            for right, parity in zip(rights, (core, 1 - core)):
                products = lax.dot_general(
                    stacked, right, (((1,), (1,)), ((), ())), preferred_element_type=jnp.float32
                )
                keep(products, parity)

    for channel in range(channels):
        one_channel(channel)


def correlate(place, own, same, other, after, previous, total_columns):
    pieces = (*own, *same, *other)
    freq_count, slab, _, depth = own[0][0].shape[1:]
    rows = freq_count * sum(array.shape[3] for array, part in own)
    in_specs = [
        pl.BlockSpec(
            (None, freq_count, CH_STEP, array.shape[3], depth),
            lambda c, p, part=part: (part, 0, c, 0, 0),
        )
        for array, part in pieces
    ]
    in_specs.append(pl.BlockSpec(memory_space=pl.ANY))
    args = [place, *[array for array, part in pieces], after]
    aliases = {}
    if previous is not None:
        aliases = {len(args): 0}
        in_specs.append(pl.BlockSpec(memory_space=pl.ANY))
        args.append(previous)
    return pl.pallas_call(
        functools.partial(correlate_kernel, (len(own), len(same), len(other))),
        grid_spec=pltpu.PrefetchScalarGridSpec(
            num_scalar_prefetch=1,
            grid=(slab // CH_STEP,),
            in_specs=in_specs,
            out_specs=[
                pl.BlockSpec((2, CH_STEP, rows, 2 * rows), lambda c, p: (0, c, 0, p[2])),
                pl.BlockSpec((8, LANES), lambda c, p: (0, 0)),
            ],
        ),
        out_shape=[
            jax.ShapeDtypeStruct((2, slab, rows, total_columns), jnp.bfloat16),
            jax.ShapeDtypeStruct((8, LANES), jnp.float32),
        ],
        input_output_aliases=aliases,
        compiler_params=pltpu.CompilerParams(vmem_limit_bytes=32 * 1024 * 1024),
        cost_estimate=pl.CostEstimate(flops=0, bytes_accessed=0, transcendentals=0),
        name="correlate",
    )(*args)


def on_device(voltages, fir_taps):
    freq_count = lax.axis_size("freq")
    tm_count = lax.axis_size("tm")
    inputs_here = voltages.shape[0]
    total_columns = inputs_here * freq_count * tm_count
    groups = inputs_here // GROUP
    widths = (1, 1, groups - 2) if groups >= 3 else (1,) * groups
    streams = len(widths)
    ring = tm_count // 2
    tm = lax.axis_index("tm").astype(jnp.int32)
    freq = lax.axis_index("freq").astype(jnp.int32)
    swap = [(i, i ^ 1) for i in range(tm_count)]
    onward = [(i, (i + 2) % tm_count) for i in range(tm_count)]

    def behind(array, *others):
        for other in others:
            array, _ = lax.optimization_barrier((array, other))
        return array

    table = folded_table(fir_taps, freq_count)
    token = jnp.zeros((8, LANES), jnp.float32)
    held, swapped = {}, {}

    def move_on(step, stream, *others):
        if (step, stream) not in held:
            array, part = held[step - 1, stream]
            piece = behind(array[part : part + 1], *others)
            held[step, stream] = (lax.ppermute(piece, "tm", onward), 0)
        return held[step, stream][0]

    def swap_cores(step, stream, *others):
        array, part = held[step, stream]
        if (step, stream) not in swapped:
            for place, (other, number) in held.items():
                if other is array and place in swapped:
                    swapped[step, stream] = (swapped[place][0], part)
        if (step, stream) not in swapped:
            swapped[step, stream] = (lax.ppermute(behind(array, *others), "tm", swap), part)

    ahead = streams == 3 and ring == 4
    first = 0
    for stream, width in enumerate(widths):
        if stream >= 2:
            token = behind(token, *[held[0, earlier][0] for earlier in range(stream)])
        spectra = channelize(voltages, table, token, first, width)
        first += width
        token = behind(token, spectra)
        spectra = spectra.reshape(freq_count, CH_DEV, width * GROUP, 2 * S)
        parts = [spectra[0]]
        for k in range(1, freq_count):
            partners = [(i, i ^ k) for i in range(freq_count)]
            parts.append(lax.ppermute(spectra[k], "freq", partners))
        if ahead and stream == 2:
            parts[-1] = behind(parts[-1], move_on(1, 1), move_on(1, 0), move_on(2, 0))
        held[0, stream] = (jnp.stack(parts)[None], 0)

    if ahead:
        both = jnp.concatenate([held[2, 0][0], held[1, 1][0]], axis=0)
        both = lax.ppermute(both, "tm", onward)
        held[3, 0], held[2, 1] = (both, 0), (both, 1)
    names = list(range(streams))
    result, tokens = None, [token]
    for step in range(ring):
        if ahead and step == 2:
            third, names = held[1, 2][0], [0, 1, 2, 3]
            middle = third.shape[3] // 2
            held[1, 2], held[1, 3] = (third[:, :, :, :middle], 0), (third[:, :, :, middle:], 0)
        for name in names:
            if step:
                others = []
                if ahead and (step, name) == (2, 2):
                    others = [tokens[1]]
                elif ahead and (step, name) == (3, 1):
                    others = [tokens[2]]
                elif ahead and (step, name) == (3, 3):
                    others = [held[3, 1][0]]
                move_on(step, name, *others)
        for name in names:
            late = step == ring - 1 and step and name == names[-1]
            swap_cores(step, name, *([tokens[-1]] if late else []))
        place = jnp.stack([freq, tm % 2, (tm // 2 + ring - step) % ring])
        result, token = correlate(
            place,
            [held[0, name] for name in range(streams)],
            [held[step, name] for name in names],
            [swapped[step, name] for name in names],
            tokens[-1],
            result,
            total_columns,
        )
        tokens.append(token)
    return result


def solution(mesh):
    placed = (P(("tm", "freq"), None), P())
    return jax.shard_map(
        on_device,
        mesh=mesh,
        in_specs=placed,
        out_specs=P(None, "freq", "tm", None),
        check_vma=False,
    )
```
